256 devices in a mesh: dp: 256 (over z, x, y, core).
Axes of the slice: x: 4, y: 4, z: 8, core: 2. Of those that a mesh axis runs over, the one named last changes fastest.
Arguments:
- audio: bfloat16 [65536, 1024], P('dp'), may hold values from -64 to 64, as said below
- text: bfloat16 [65536, 1024], P('dp'), may hold values from -64 to 64, as said below
- log_scale: float32 [1], replicated, may hold values from 3.7 to 4.4
- bias: float32 [1], replicated, may hold values from -4 to -2
- plan: int32 [256, 3], P('dp'), may hold values from 0 to 255, as said below
Outputs:
- row_loss: float32 [65536], P('dp')
- grad_audio: float32 [65536, 1024], P('dp')
- grad_text: float32 [65536, 1024], P('dp')
- stats: float32 [3], replicated
The draws below stay inside these ranges and needn't reach their ends.
Inputs may be any that keep to these rules, and one draw needn't show every extreme that they name: `plan`: the partner of player g in round r is (g + s_r) mod 256, where s_r lies in 1 .. 255, is the same for every player, and differs between rounds. Rows of audio have differing norms; every row is nonzero. Rows of text have differing norms; every row is nonzero.
All inputs are finite; a program needn't handle non-finite values.
Results may differ from the reference program's by a relative error of at most 0.0022.
Values may be sent and summed in bfloat16 or wider, within the bound.
A program may use at most 320 MiB of HBM per device.

```python
import jax
import jax.numpy as jnp
from jax import lax

D = 1024
TOK_DEV = 256
ROUNDS = 3
TOKENS = 65536
N_DP = 256


def shared_latent(key):
    latent = jax.random.normal(key, (TOKENS, D), jnp.float32)
    common = jax.random.normal(jax.random.fold_in(key, 5), (1, D), jnp.float32)
    return (latent, common)


def ramp_rows(top):
    position = jnp.arange(TOKENS, dtype=jnp.float32)[:, None] / float(TOKENS)
    return top * position


def draw_audio(key, part):
    latent, common = shared_latent(key)
    key = jax.random.fold_in(key, 11)
    noise_key, scale_key = jax.random.split(key, 2)
    noise_rows = jax.random.normal(noise_key, (TOKENS, D), jnp.float32)
    scales = jax.random.uniform(scale_key, (TOKENS, 1), jnp.float32, 0.5, 2.0)
    offset = ramp_rows(0.3) * common
    return jnp.clip((noise_rows + 0.4 * latent + offset) * scales, -64.0, 64.0).astype(jnp.bfloat16)


def draw_text(key, part):
    latent, common = shared_latent(key)
    key = jax.random.fold_in(key, 23)
    noise_key, scale_key = jax.random.split(key, 2)
    noise_rows = jax.random.normal(noise_key, (TOKENS, D), jnp.float32)
    scales = jax.random.uniform(scale_key, (TOKENS, 1), jnp.float32, 0.5, 2.0)
    offset = ramp_rows(0.3) * common
    return jnp.clip((noise_rows + 0.4 * latent + offset) * scales, -64.0, 64.0).astype(jnp.bfloat16)


def draw_plan(key, part):
    key = jax.random.fold_in(key, 37)
    round_shifts = jax.random.permutation(key, N_DP - 1)[:ROUNDS].astype(jnp.int32) + 1
    players = jnp.arange(N_DP, dtype=jnp.int32)
    return jnp.remainder(players[:, None] + round_shifts[None, :], N_DP).astype(jnp.int32)


def setup_inputs(seed: int = 0) -> dict:
    key_list = jax.random.split(jax.random.key(seed), 6)
    return {
        "audio": draw_audio(jax.random.fold_in(key_list[5], 71), 0),
        "text": draw_text(jax.random.fold_in(key_list[5], 71), 0),
        "log_scale": jnp.clip(jax.random.uniform(key_list[2], (1,), jnp.float32, 3.7, 4.4), 3.7, 4.4),
        "bias": jnp.clip(jax.random.uniform(key_list[3], (1,), jnp.float32, -4.0, -2.0), -4.0, -2.0),
        "plan": draw_plan(jax.random.fold_in(key_list[5], 71), 0),
    }


EPSILON = 1e-06

def unit_rows(raw_rows):
    widened = raw_rows.astype(jnp.float32)
    reciprocal = lax.rsqrt(lax.optimization_barrier(jnp.sum(widened * widened, axis=-1, keepdims=True)) + EPSILON)
    return (widened * reciprocal, reciprocal)

def block_logits(left_rows, right_rows, logit_scale, logit_bias, positive):
    cosine = jnp.dot(left_rows, right_rows.T, preferred_element_type=jnp.float32)
    logits = logit_scale * cosine + logit_bias
    diagonal = positive * jnp.eye(left_rows.shape[0], dtype=jnp.float32)
    labels = 2.0 * diagonal - 1.0
    losses = -jax.nn.log_sigmoid(labels * logits)
    slopes = jax.nn.sigmoid(logits) - diagonal
    weights = (logit_scale * slopes).astype(jnp.bfloat16)
    block_sums = jnp.stack([jnp.sum(losses), jnp.sum(slopes), jnp.sum(slopes * (logits - logit_bias))])
    return (lax.optimization_barrier(jnp.sum(losses, axis=1)), weights, block_sums)

def reference(audio, text, log_scale, bias, plan):
    audio_wide, audio_recip = unit_rows(audio)
    text_wide, text_recip = unit_rows(text)
    audio_unit = audio_wide.astype(jnp.bfloat16)
    text_unit = text_wide.astype(jnp.bfloat16)
    logit_scale = jnp.exp(log_scale[0])
    logit_bias = bias[0]
    audio_blocks = audio_unit.reshape(N_DP, TOK_DEV, D)
    text_blocks = text_unit.reshape(N_DP, TOK_DEV, D)

    def visit_player(carried, player):
        text_grad, totals = carried
        own_audio = audio_blocks[player]
        own_text = text_blocks[player]
        row_sums, weights, block_sums = block_logits(own_audio, own_text, logit_scale, logit_bias, 1.0)
        audio_grad = jnp.dot(weights, own_text, preferred_element_type=jnp.float32)
        text_grad = text_grad.at[player].add(jnp.dot(weights.T, own_audio, preferred_element_type=jnp.float32))
        totals = totals + block_sums
        for round_index in range(ROUNDS):
            partner = plan[player, round_index]
            far_text = text_blocks[partner]
            part_sums, weights, block_sums = block_logits(own_audio, far_text, logit_scale, logit_bias, 0.0)
            row_sums = row_sums + part_sums
            audio_grad = audio_grad + jnp.dot(weights, far_text, preferred_element_type=jnp.float32)
            partial_grad = lax.optimization_barrier(jnp.dot(weights.T, own_audio, preferred_element_type=jnp.float32).astype(jnp.bfloat16))
            text_grad = text_grad.at[partner].add(partial_grad.astype(jnp.float32))
            totals = totals + block_sums
        return ((text_grad, totals), (row_sums, audio_grad))
    initial = (jnp.zeros((N_DP, TOK_DEV, D), jnp.float32), jnp.zeros((3,), jnp.float32))
    (text_grad, totals), (row_loss, audio_grad) = lax.scan(visit_player, initial, jnp.arange(N_DP, dtype=jnp.int32))
    audio_grad = audio_grad.reshape(TOKENS, D)
    text_grad = text_grad.reshape(TOKENS, D)
    grad_audio = audio_recip * (audio_grad - audio_wide * lax.optimization_barrier(jnp.sum(audio_wide * audio_grad, axis=-1, keepdims=True)))
    grad_text = text_recip * (text_grad - text_wide * lax.optimization_barrier(jnp.sum(text_wide * text_grad, axis=-1, keepdims=True)))
    stats = totals / float((ROUNDS + 1) * TOK_DEV * TOKENS)
    return (row_loss.reshape(TOKENS), grad_audio, grad_text, stats)
```

```python
from functools import partial

import jax
import jax.numpy as jnp
import numpy as np
from jax import lax
from jax.experimental import pallas as pl
from jax.experimental.pallas import tpu as pltpu
from jax.sharding import PartitionSpec as P

EPSILON = 1e-06
ROUNDS = 3
HALF = 128
BRANCHES = (8, 4, 4)
STAGES = ((1, 8), (8, 4), (32, 8))
MESH = pl.DeviceIdType.MESH


def shift_costs():
    return np.array(COST, np.int32)


COST = [112, 165, 217, 270, 217, 165, 151, 165, 178, 191, 217, 270, 230, 243, 256, 270, 256, 243, 230, 270, 217, 191, 178, 165, 151, 165, 217, 270, 217, 165, 161, 165, 168, 171, 217, 270, 217, 184, 187, 191, 194, 197, 217, 270, 230, 243, 256, 270, 256, 243, 230, 270, 233, 237, 240, 243, 247, 250, 253, 270, 260, 263, 266, 270, 273, 276, 279, 283, 286, 289, 292, 296, 299, 302, 306, 309, 312, 315, 319, 322, 325, 329, 332, 335, 338, 342, 345, 348, 352, 355, 358, 361, 365, 368, 371, 375, 378, 381, 384, 388, 391, 394, 397, 401, 404, 407, 411, 414, 417, 420, 424, 427, 430, 434, 437, 440, 443, 447, 450, 453, 457, 460, 463, 466, 470, 473, 476, 480]


def schedule_kernel(plan_ref, cost_ref, out_ref):
    me = lax.axis_index("dp")
    offsets = [(plan_ref[0, r] - me) & 255 for r in range(ROUNDS)]

    def cost(distance):
        return cost_ref[jnp.maximum(jnp.minimum(distance, 256 - distance) - 1, 0)]

    far = jnp.int32(1 << 28)
    best = [cost(s) for s in offsets]
    parent = [jnp.int32(0)] * ROUNDS
    step_of = list(offsets)
    done = [jnp.int32(0)] * ROUNDS
    for step in range(ROUNDS):
        keys = [jnp.where(done[j] == 1, far, best[j]) for j in range(ROUNDS)]
        first = (keys[0] <= keys[1]) & (keys[0] <= keys[2])
        pick = jnp.where(first, 0, jnp.where(keys[1] <= keys[2], 1, 2))

        def chosen(values):
            return jnp.where(pick == 0, values[0], jnp.where(pick == 1, values[1], values[2]))

        distance = chosen(step_of)
        at = chosen(offsets)
        wrapped = jnp.where(distance <= HALF, 0, 1)
        out_ref[4 * step] = chosen(parent)
        out_ref[4 * step + 1] = jnp.maximum(jnp.minimum(distance, 256 - distance) - 1, 0)
        out_ref[4 * step + 2] = wrapped
        out_ref[4 * step + 3] = 0
        for j in range(ROUNDS):
            done[j] = jnp.where(pick == j, 1, done[j])
            onward = (offsets[j] - at) & 255
            price = cost(onward)
            nearer = price < best[j]
            best[j] = jnp.where(nearer, price, best[j])
            parent[j] = jnp.where(nearer, step + 1, parent[j])
            step_of[j] = jnp.where(nearer, onward, step_of[j])


def make_schedule(plan):
    return pl.pallas_call(
        schedule_kernel,
        out_shape=jax.ShapeDtypeStruct((4 * ROUNDS,), jnp.int32),
        in_specs=[pl.BlockSpec(memory_space=pltpu.SMEM)] * 2,
        out_specs=pl.BlockSpec(memory_space=pltpu.SMEM),
    )(plan, jnp.asarray(shift_costs()))


def both_ways(distance, blocks):
    ahead, back = blocks
    peers = lax.axis_size("dp")
    return (
        lax.ppermute(ahead, "dp", [(i, (i + distance) % peers) for i in range(peers)]),
        lax.ppermute(back, "dp", [(i, (i - distance) % peers) for i in range(peers)]),
    )


def exchange(distances, digits, widths, blocks):
    if not widths:
        return both_ways(distances[0], blocks)
    count = len(distances) // widths[0]
    branches = [
        partial(exchange, distances[i * count : (i + 1) * count], digits[1:], widths[1:])
        for i in range(widths[0])
    ]
    return lax.switch(digits[0], branches, blocks)


def unit_rows(raw):
    wide = raw.astype(jnp.float32)
    recip = lax.rsqrt(jnp.sum(wide * wide, axis=-1, keepdims=True) + EPSILON)
    wide = wide * recip
    return wide, recip, wide.astype(jnp.bfloat16)


def dot_t(a, b):
    return lax.dot_general(a, b, (((1,), (1,)), ((), ())), preferred_element_type=jnp.float32)


def project(wide, recip, grad):
    along = jnp.sum(wide * grad, axis=-1, keepdims=True)
    return recip * (grad - wide * along)


def loss_kernel(scale_ref, bias_ref, held_ref, row_ref, ga_ref, gt_ref, tot_ref):
    scale = jnp.exp(jnp.full((1, 1), scale_ref[0], jnp.float32))
    bias = bias_ref[0]
    n = held_ref.shape[2]
    rows = lax.broadcasted_iota(jnp.int32, (n, n), 0)
    cols = lax.broadcasted_iota(jnp.int32, (n, n), 1)
    eye = (rows == cols).astype(jnp.float32)

    audio_wide, audio_recip, audio_unit = unit_rows(held_ref[0, 0])
    text_wide, text_recip, text_unit = unit_rows(held_ref[0, 1])
    losses_sum = jnp.zeros((n, n), jnp.float32)
    slopes_sum = jnp.zeros((n, n), jnp.float32)
    scaled_sum = jnp.zeros((n, n), jnp.float32)
    audio_grad = jnp.zeros(audio_wide.shape, jnp.float32)
    text_grad = jnp.zeros(text_wide.shape, jnp.float32)
    for slot in range(ROUNDS + 1):
        far_text = text_unit if slot == 0 else unit_rows(held_ref[slot, 1])[2]
        far_audio = audio_unit if slot == 0 else unit_rows(held_ref[slot, 0])[2]
        scaled = scale * dot_t(audio_unit, far_text)
        logits = scaled + bias
        small = jnp.exp(-jnp.abs(logits))
        slopes = jnp.where(logits >= 0.0, 1.0, small) / (1.0 + small)
        if slot == 0:
            flipped = jnp.where(rows == cols, -logits, logits)
            slopes = slopes - eye
        else:
            flipped = logits
        losses_sum = losses_sum + (jnp.maximum(flipped, 0.0) + jnp.log1p(small))
        slopes_sum = slopes_sum + slopes
        scaled_sum = scaled_sum + slopes * scaled
        weights = (scale * slopes).astype(jnp.bfloat16)
        audio_grad = audio_grad + jnp.dot(weights, far_text, preferred_element_type=jnp.float32)

        logits = scale * dot_t(text_unit, far_audio) + bias
        small = jnp.exp(-jnp.abs(logits))
        slopes = jnp.where(logits >= 0.0, 1.0, small) / (1.0 + small)
        if slot == 0:
            slopes = slopes - eye
        weights = (scale * slopes).astype(jnp.bfloat16)
        text_grad = text_grad + jnp.dot(weights, far_audio, preferred_element_type=jnp.float32)

    ga_ref[...] = project(audio_wide, audio_recip, audio_grad)
    gt_ref[...] = project(text_wide, text_recip, text_grad)
    folded = losses_sum[:, : n // 2] + losses_sum[:, n // 2 :]
    row_ref[...] = jnp.sum(folded.T, axis=0, keepdims=True)
    parts = []
    for total in (losses_sum, slopes_sum, scaled_sum):
        down = jnp.sum(total, axis=0, keepdims=True)
        parts.append(down[:, : n // 2] + down[:, n // 2 :])
    tot_ref[...] = jnp.concatenate(parts + [jnp.zeros((5, n // 2), jnp.float32)], axis=0)


def loss_and_grads(log_scale, bias, held):
    n, d = held.shape[2:]
    vmem = pl.BlockSpec(memory_space=pltpu.VMEM)
    smem = pl.BlockSpec(memory_space=pltpu.SMEM)
    return pl.pallas_call(
        loss_kernel,
        out_shape=(
            jax.ShapeDtypeStruct((1, n), jnp.float32),
            jax.ShapeDtypeStruct((n, d), jnp.float32),
            jax.ShapeDtypeStruct((n, d), jnp.float32),
            jax.ShapeDtypeStruct((8, n // 2), jnp.float32),
        ),
        in_specs=[smem, smem, vmem],
        out_specs=(vmem, vmem, vmem, vmem),
        compiler_params=pltpu.CompilerParams(vmem_limit_bytes=48 * 1024 * 1024),
    )(log_scale, bias, held)


def stats_kernel(denominator, part_ref, out_ref, *scratch):
    me = lax.axis_index("dp")
    buffers, sends, recvs = scratch[0:3], scratch[3:6], scratch[6:9]
    groups = []
    for stride, peers in STAGES:
        digit = lax.rem(lax.div(me, stride), peers)
        others = []
        for k in range(1, peers):
            other = lax.rem(digit + k, peers)
            others.append((other, me + (other - digit) * stride))
        groups.append((digit, others))
    barrier = pltpu.get_barrier_semaphore()
    count = 0
    for _, others in groups:
        for _, device in others:
            pl.semaphore_signal(barrier, inc=1, device_id=(device,), device_id_type=MESH)
            count += 1
    pl.semaphore_wait(barrier, count)
    value = part_ref[...]
    for stage, (digit, others) in enumerate(groups):
        buffer, send, recv = buffers[stage], sends[stage], recvs[stage]
        buffer[digit] = value
        for other, device in others:
            pltpu.make_async_remote_copy(
                src_ref=buffer.at[digit],
                dst_ref=buffer.at[digit],
                send_sem=send.at[other],
                recv_sem=recv.at[digit],
                device_id=(device,),
                device_id_type=MESH,
            ).start()
        for other, device in others:
            arrived = pltpu.make_async_remote_copy(
                src_ref=buffer.at[digit],
                dst_ref=buffer.at[other],
                send_sem=send.at[other],
                recv_sem=recv.at[other],
                device_id=(device,),
                device_id_type=MESH,
            )
            arrived.wait_recv()
            arrived.wait_send()
        value = buffer[0]
        for j in range(1, STAGES[stage][1]):
            value = value + buffer[j]
    total = jnp.sum(value, axis=1, keepdims=True) / denominator
    out_ref[...] = jnp.broadcast_to(total, out_ref.shape)


def all_stats(parts, denominator):
    vmem = pl.BlockSpec(memory_space=pltpu.VMEM)
    scratch = [pltpu.VMEM((peers,) + parts.shape, jnp.float32) for _, peers in STAGES]
    scratch += [pltpu.SemaphoreType.DMA((peers,)) for _, peers in STAGES] * 2
    return pl.pallas_call(
        partial(stats_kernel, denominator),
        out_shape=jax.ShapeDtypeStruct(parts.shape, jnp.float32),
        in_specs=[vmem],
        out_specs=vmem,
        scratch_shapes=scratch,
        compiler_params=pltpu.CompilerParams(collective_id=0, has_side_effects=True),
    )(parts)[:3, 0]


def local(audio, text, log_scale, bias, plan):
    n, d = audio.shape
    player_count = lax.axis_size("dp")
    steps = make_schedule(plan)
    held = jnp.zeros((ROUNDS + 1, 2, n, d), audio.dtype)
    held = held.at[0, 0].set(audio).at[0, 1].set(text)

    def fetch(step, held):
        parent, branch, wrapped = [steps[4 * step + i] for i in range(3)]
        blocks = (held[parent, wrapped], held[parent, 1 - wrapped])
        digits = []
        for width in reversed(BRANCHES):
            digits.insert(0, lax.rem(branch, width))
            branch = lax.div(branch, width)
        ahead, back = exchange(list(range(1, HALF + 1)), digits, BRANCHES, blocks)
        held = held.at[step + 1, wrapped].set(ahead)
        return held.at[step + 1, 1 - wrapped].set(back)

    held = lax.fori_loop(0, ROUNDS, fetch, held)
    row_loss, grad_audio, grad_text, parts = loss_and_grads(log_scale, bias, held)
    stats = all_stats(parts, float((ROUNDS + 1) * n * n * player_count))
    return (row_loss.reshape(n), grad_audio, grad_text, stats)


def solution(mesh):
    return jax.shard_map(
        local,
        mesh=mesh,
        in_specs=(P("dp", None), P("dp", None), P(), P(), P("dp", None)),
        out_specs=(P("dp"), P("dp", None), P("dp", None), P()),
        check_vma=False,
    )
```

```python
from functools import partial

import jax
import jax.numpy as jnp
import numpy as np
from jax import lax
from jax.experimental import pallas as pl
from jax.experimental.pallas import tpu as pltpu
from jax.sharding import PartitionSpec as P

EPSILON = 1e-06
ROUNDS = 3
HALF = 128
STAGES = ((1, 8), (8, 4), (32, 8))
MESH = pl.DeviceIdType.MESH

SHIFTS = (1, 2, 3, 4, 5, 6, 7, 8, 9, 10, 11, 12, 13, 14, 15, 16, 17, 18, 19, 20, 21, 22, 23, 24, 25, 26, 27, 28, 29, 30, 31, 32, 64, 96)
WIDTH = 6
COST = [156, 211, 216, 234, 232, 215, 210, 213, 220, 262, 270, 295, 292, 274, 280, 241, 258, 231, 242, 269, 253, 284, 240, 216, 223, 226, 239, 283, 249, 238, 234, 212, 369, 423, 428, 446, 444, 427, 422, 425, 433, 447, 454, 457, 468, 476, 456, 431, 439, 441, 449, 451, 464, 454, 450, 428, 435, 438, 451, 476, 461, 450, 447, 339, 495, 550, 555, 573, 571, 554, 549, 552, 559, 600, 609, 634, 631, 613, 619, 580, 597, 570, 581, 608, 592, 623, 579, 555, 562, 565, 578, 622, 588, 577, 573, 453, 609, 664, 669, 687, 685, 668, 663, 666, 673, 715, 723, 748, 745, 727, 734, 694, 711, 684, 695, 722, 706, 737, 693, 669, 676, 679, 692, 736, 702, 691, 687, 666]
FIRST = [0, 2, 4, 6, 8, 10, 12, 14, 16, 18, 20, 22, 24, 26, 28, 30, 32, 34, 36, 38, 40, 42, 44, 46, 48, 50, 52, 54, 56, 58, 60, 62, 0, 2, 4, 6, 8, 10, 12, 14, 16, 34, 34, 34, 36, 40, 44, 46, 46, 46, 48, 50, 46, 46, 46, 46, 48, 50, 52, 58, 56, 58, 60, 64, 0, 2, 4, 6, 8, 10, 12, 14, 16, 18, 20, 22, 24, 26, 28, 30, 32, 34, 36, 38, 40, 42, 44, 46, 48, 50, 52, 54, 56, 58, 60, 66, 0, 2, 4, 6, 8, 10, 12, 14, 16, 18, 20, 22, 24, 26, 28, 30, 32, 34, 36, 38, 40, 42, 44, 46, 48, 50, 52, 54, 56, 58, 60, 62]
SECOND = [-1, -1, -1, -1, -1, -1, -1, -1, -1, -1, -1, -1, -1, -1, -1, -1, -1, -1, -1, -1, -1, -1, -1, -1, -1, -1, -1, -1, -1, -1, -1, -1, 62, 62, 62, 62, 62, 62, 62, 62, 62, 46, 48, 50, 50, 48, 46, 46, 48, 50, 50, 50, 56, 58, 60, 62, 62, 62, 62, 58, 62, 62, 62, -1, 64, 64, 64, 64, 64, 64, 64, 64, 64, 64, 64, 64, 64, 64, 64, 64, 64, 64, 64, 64, 64, 64, 64, 64, 64, 64, 64, 64, 64, 64, 64, -1, 66, 66, 66, 66, 66, 66, 66, 66, 66, 66, 66, 66, 66, 66, 66, 66, 66, 66, 66, 66, 66, 66, 66, 66, 66, 66, 66, 66, 66, 66, 66, 66]


def plan_kernel(plan_ref, table_ref, audio_ref, text_ref, held_ref, code_ref, count_ref, sems):
    own = [
        pltpu.make_async_copy(ref, held_ref.at[i], sems.at[i])
        for i, ref in enumerate((audio_ref, text_ref))
    ]
    for copy in own:
        copy.start()
    me = lax.axis_index("dp")
    offsets = [(plan_ref[0, r] - me) & 255 for r in range(ROUNDS)]

    def entry(distance):
        return jnp.maximum(jnp.minimum(distance, 256 - distance) - 1, 0)

    def cost(distance):
        return table_ref[entry(distance)]

    def write(at, transfer, source, target):
        leaf = transfer >> 1
        back = transfer & 1
        high = lax.div(leaf, WIDTH)
        code_ref[at] = (
            high
            | ((leaf - high * WIDTH) << 4)
            | ((2 * source + back) << 8)
            | ((2 * source + 1 - back) << 12)
            | ((2 * target + back) << 16)
            | ((2 * target + 1 - back) << 20)
        )

    far = jnp.int32(1 << 28)
    best = [cost(s) for s in offsets]
    parent = [jnp.int32(0)] * ROUNDS
    away = list(offsets)
    done = [jnp.int32(0)] * ROUNDS
    count = jnp.int32(0)
    for step in range(ROUNDS):
        keys = [jnp.where(done[j] == 1, far, best[j]) for j in range(ROUNDS)]
        first = (keys[0] <= keys[1]) & (keys[0] <= keys[2])
        pick = jnp.where(first, 0, jnp.where(keys[1] <= keys[2], 1, 2))

        def chosen(values):
            return jnp.where(pick == 0, values[0], jnp.where(pick == 1, values[1], values[2]))

        distance = chosen(away)
        at = chosen(offsets)
        mirrored = jnp.where(distance <= HALF, 0, 1)
        one = table_ref[HALF + entry(distance)]
        two = table_ref[2 * HALF + entry(distance)]
        write(count, one ^ mirrored, chosen(parent), step + 1)
        write(count + 1, jnp.maximum(two, 0) ^ mirrored, jnp.int32(step + 1), step + 1)
        count = count + jnp.where(two >= 0, 2, 1)
        for j in range(ROUNDS):
            done[j] = jnp.where(pick == j, 1, done[j])
            onward = (offsets[j] - at) & 255
            price = cost(onward)
            nearer = price < best[j]
            best[j] = jnp.where(nearer, price, best[j])
            parent[j] = jnp.where(nearer, step + 1, parent[j])
            away[j] = jnp.where(nearer, onward, away[j])
    count_ref[0] = count
    for copy in own:
        copy.wait()


def plan_transfers(audio, text, plan):
    smem = pl.BlockSpec(memory_space=pltpu.SMEM)
    anywhere = pl.BlockSpec(memory_space=pl.ANY)
    return pl.pallas_call(
        plan_kernel,
        out_shape=(
            jax.ShapeDtypeStruct((2 * (ROUNDS + 1),) + audio.shape, audio.dtype),
            jax.ShapeDtypeStruct((8,), jnp.int32),
            jax.ShapeDtypeStruct((1,), jnp.int32),
        ),
        in_specs=[smem, smem, anywhere, anywhere],
        out_specs=(anywhere, smem, smem),
        scratch_shapes=[pltpu.SemaphoreType.DMA((2,))],
    )(plan, jnp.asarray(np.array(COST + FIRST + SECOND, np.int32)), audio, text)


def swap_kernel(distance, ahead_ref, back_ref, ahead_out, back_out, send_sem, recv_sem):
    me = lax.axis_index("dp")
    after = lax.rem(me + distance, 256)
    before = lax.rem(me + 256 - distance, 256)
    barrier = pltpu.get_barrier_semaphore()
    for device in (after, before):
        pl.semaphore_signal(barrier, inc=1, device_id=(device,), device_id_type=MESH)
    pl.semaphore_wait(barrier, 2)
    copies = [
        pltpu.make_async_remote_copy(
            src_ref=src,
            dst_ref=dst,
            send_sem=send_sem.at[i],
            recv_sem=recv_sem.at[i],
            device_id=(device,),
            device_id_type=MESH,
        )
        for i, (src, dst, device) in enumerate(
            ((ahead_ref, ahead_out, after), (back_ref, back_out, before))
        )
    ]
    for copy in copies:
        copy.start()
    for copy in copies:
        copy.wait()


def both_ways(leaf, blocks):
    anywhere = pl.BlockSpec(memory_space=pl.ANY)
    return pl.pallas_call(
        partial(swap_kernel, SHIFTS[leaf]),
        out_shape=[jax.ShapeDtypeStruct(b.shape, b.dtype) for b in blocks],
        in_specs=[anywhere] * 2,
        out_specs=[anywhere] * 2,
        scratch_shapes=[pltpu.SemaphoreType.DMA((2,)), pltpu.SemaphoreType.DMA((2,))],
        compiler_params=pltpu.CompilerParams(collective_id=1 + leaf, has_side_effects=True),
    )(*blocks)


def exchange(high, low, blocks):
    def group(i, blocks):
        leaves = range(i * WIDTH, min((i + 1) * WIDTH, len(SHIFTS)))
        return lax.switch(low, [partial(both_ways, leaf) for leaf in leaves], blocks)

    return lax.switch(high, [partial(group, i) for i in range(-(-len(SHIFTS) // WIDTH))], blocks)


def unit_rows(raw):
    wide = raw.astype(jnp.float32)
    recip = lax.rsqrt(jnp.sum(wide * wide, axis=-1, keepdims=True) + EPSILON)
    wide = wide * recip
    return wide, recip, wide.astype(jnp.bfloat16)


def dot_t(a, b):
    return lax.dot_general(a, b, (((1,), (1,)), ((), ())), preferred_element_type=jnp.float32)


def project(wide, recip, grad):
    along = jnp.sum(wide * grad, axis=-1, keepdims=True)
    return recip * (grad - wide * along)


def loss_kernel(scale_ref, bias_ref, held_ref, row_ref, ga_ref, gt_ref, tot_ref):
    scale = jnp.exp(jnp.full((1, 1), scale_ref[0], jnp.float32))
    bias = bias_ref[0]
    n = held_ref.shape[1]
    rows = lax.broadcasted_iota(jnp.int32, (n, n), 0)
    cols = lax.broadcasted_iota(jnp.int32, (n, n), 1)
    eye = (rows == cols).astype(jnp.float32)

    audio_wide, audio_recip, audio_unit = unit_rows(held_ref[0])
    text_wide, text_recip, text_unit = unit_rows(held_ref[1])
    losses_sum = jnp.zeros((n, n), jnp.float32)
    slopes_sum = jnp.zeros((n, n), jnp.float32)
    scaled_sum = jnp.zeros((n, n), jnp.float32)
    audio_grad = jnp.zeros(audio_wide.shape, jnp.float32)
    text_grad = jnp.zeros(text_wide.shape, jnp.float32)
    for slot in range(ROUNDS + 1):
        far_text = text_unit if slot == 0 else unit_rows(held_ref[2 * slot + 1])[2]
        far_audio = audio_unit if slot == 0 else unit_rows(held_ref[2 * slot])[2]
        scaled = scale * dot_t(audio_unit, far_text)
        logits = scaled + bias
        small = jnp.exp(-jnp.abs(logits))
        slopes = jnp.where(logits >= 0.0, 1.0, small) / (1.0 + small)
        if slot == 0:
            flipped = jnp.where(rows == cols, -logits, logits)
            slopes = slopes - eye
        else:
            flipped = logits
        losses_sum = losses_sum + (jnp.maximum(flipped, 0.0) + jnp.log1p(small))
        slopes_sum = slopes_sum + slopes
        scaled_sum = scaled_sum + slopes * scaled
        weights = (scale * slopes).astype(jnp.bfloat16)
        audio_grad = audio_grad + jnp.dot(weights, far_text, preferred_element_type=jnp.float32)

        logits = scale * dot_t(text_unit, far_audio) + bias
        small = jnp.exp(-jnp.abs(logits))
        slopes = jnp.where(logits >= 0.0, 1.0, small) / (1.0 + small)
        if slot == 0:
            slopes = slopes - eye
        weights = (scale * slopes).astype(jnp.bfloat16)
        text_grad = text_grad + jnp.dot(weights, far_audio, preferred_element_type=jnp.float32)

    ga_ref[...] = project(audio_wide, audio_recip, audio_grad)
    gt_ref[...] = project(text_wide, text_recip, text_grad)
    folded = losses_sum[:, : n // 2] + losses_sum[:, n // 2 :]
    row_ref[...] = jnp.sum(folded.T, axis=0, keepdims=True)
    parts = []
    for total in (losses_sum, slopes_sum, scaled_sum):
        down = jnp.sum(total, axis=0, keepdims=True)
        parts.append(down[:, : n // 2] + down[:, n // 2 :])
    tot_ref[...] = jnp.concatenate(parts + [jnp.zeros((5, n // 2), jnp.float32)], axis=0)


def loss_and_grads(log_scale, bias, held):
    n, d = held.shape[1:]
    vmem = pl.BlockSpec(memory_space=pltpu.VMEM)
    smem = pl.BlockSpec(memory_space=pltpu.SMEM)
    return pl.pallas_call(
        loss_kernel,
        out_shape=(
            jax.ShapeDtypeStruct((1, n), jnp.float32),
            jax.ShapeDtypeStruct((n, d), jnp.float32),
            jax.ShapeDtypeStruct((n, d), jnp.float32),
            jax.ShapeDtypeStruct((8, n // 2), jnp.float32),
        ),
        in_specs=[smem, smem, vmem],
        out_specs=(vmem, vmem, vmem, vmem),
        compiler_params=pltpu.CompilerParams(vmem_limit_bytes=48 * 1024 * 1024),
    )(log_scale, bias, held)


def stats_kernel(denominator, part_ref, out_ref, *scratch):
    me = lax.axis_index("dp")
    buffers, sends, recvs = scratch[0:3], scratch[3:6], scratch[6:9]
    groups = []
    for stride, peers in STAGES:
        digit = lax.rem(lax.div(me, stride), peers)
        others = []
        for k in range(1, peers):
            other = lax.rem(digit + k, peers)
            others.append((other, me + (other - digit) * stride))
        groups.append((digit, others))
    barrier = pltpu.get_barrier_semaphore()
    count = 0
    for _, others in groups:
        for _, device in others:
            pl.semaphore_signal(barrier, inc=1, device_id=(device,), device_id_type=MESH)
            count += 1
    pl.semaphore_wait(barrier, count)
    value = part_ref[...]
    for stage, (digit, others) in enumerate(groups):
        buffer, send, recv = buffers[stage], sends[stage], recvs[stage]
        buffer[digit] = value
        for other, device in others:
            pltpu.make_async_remote_copy(
                src_ref=buffer.at[digit],
                dst_ref=buffer.at[digit],
                send_sem=send.at[other],
                recv_sem=recv.at[digit],
                device_id=(device,),
                device_id_type=MESH,
            ).start()
        for other, device in others:
            arrived = pltpu.make_async_remote_copy(
                src_ref=buffer.at[digit],
                dst_ref=buffer.at[other],
                send_sem=send.at[other],
                recv_sem=recv.at[other],
                device_id=(device,),
                device_id_type=MESH,
            )
            arrived.wait_recv()
            arrived.wait_send()
        value = buffer[0]
        for j in range(1, STAGES[stage][1]):
            value = value + buffer[j]
    total = jnp.sum(value, axis=1, keepdims=True) / denominator
    out_ref[...] = jnp.broadcast_to(total, out_ref.shape)


def all_stats(parts, denominator):
    vmem = pl.BlockSpec(memory_space=pltpu.VMEM)
    scratch = [pltpu.VMEM((peers,) + parts.shape, jnp.float32) for _, peers in STAGES]
    scratch += [pltpu.SemaphoreType.DMA((peers,)) for _, peers in STAGES] * 2
    return pl.pallas_call(
        partial(stats_kernel, denominator),
        out_shape=jax.ShapeDtypeStruct(parts.shape, jnp.float32),
        in_specs=[vmem],
        out_specs=vmem,
        scratch_shapes=scratch,
        compiler_params=pltpu.CompilerParams(collective_id=0, has_side_effects=True),
    )(parts)[:3, 0]


def local(audio, text, log_scale, bias, plan):
    n = audio.shape[0]
    player_count = lax.axis_size("dp")
    held, codes, count = plan_transfers(audio, text, plan)

    def fetch(step, held):
        code = lax.dynamic_index_in_dim(codes, step, keepdims=False)
        high, low, *at = [(code >> (4 * i)) & 15 for i in range(6)]
        blocks = [lax.dynamic_index_in_dim(held, i, keepdims=False) for i in at[:2]]
        for block, i in zip(exchange(high, low, blocks), at[2:]):
            held = lax.dynamic_update_index_in_dim(held, block, i, 0)
        return held

    held = lax.fori_loop(0, count[0], fetch, held)
    row_loss, grad_audio, grad_text, parts = loss_and_grads(log_scale, bias, held)
    stats = all_stats(parts, float((ROUNDS + 1) * n * n * player_count))
    return (row_loss.reshape(n), grad_audio, grad_text, stats)


def solution(mesh):
    return jax.shard_map(
        local,
        mesh=mesh,
        in_specs=(P("dp", None), P("dp", None), P(), P(), P("dp", None)),
        out_specs=(P("dp"), P("dp", None), P("dp", None), P()),
        check_vma=False,
    )
```

```python
from functools import partial

import jax
import jax.numpy as jnp
import numpy as np
from jax import lax
from jax.experimental import pallas as pl
from jax.experimental.pallas import tpu as pltpu
from jax.sharding import PartitionSpec as P

EPSILON = 1e-06
ROUNDS = 3
HALF = 128
STAGES = ((1, 8), (8, 4), (32, 8))
MESH = pl.DeviceIdType.MESH
MIB = 1024 * 1024

SHIFTS = (1, 2, 3, 4, 6, 7, 9, 10, 11, 14, 15, 16, 17, 18, 19, 20, 21, 23, 24, 26, 27, 29, 30, 32, 33, 40, 46, 57, 59, 63, 64, 65, 73, 91, 128)
COST = [156, 211, 216, 234, 371, 215, 210, 366, 220, 262, 270, 426, 424, 274, 280, 241, 258, 231, 242, 269, 253, 397, 240, 216, 372, 226, 239, 395, 249, 238, 369, 212, 271, 423, 428, 446, 448, 427, 422, 335, 433, 447, 458, 457, 468, 359, 456, 431, 466, 441, 454, 451, 464, 454, 453, 428, 347, 438, 363, 476, 461, 450, 358, 339, 388, 541, 555, 573, 572, 554, 549, 547, 462, 600, 579, 590, 594, 571, 599, 580, 563, 570, 573, 586, 589, 596, 573, 555, 560, 565, 477, 606, 588, 577, 570, 551, 601, 659, 688, 697, 708, 695, 693, 674, 674, 733, 718, 735, 708, 698, 728, 711, 750, 695, 693, 711, 703, 716, 690, 705, 679, 684, 689, 703, 685, 680, 626, 469]
FIRST = [0, 2, 4, 6, 1, 8, 10, 0, 12, 14, 16, 0, 8, 18, 20, 22, 24, 26, 28, 30, 32, 1, 34, 36, 0, 38, 40, 0, 42, 44, 1, 46, 48, 2, 4, 6, 10, 8, 10, 50, 12, 26, 28, 26, 28, 52, 34, 36, 34, 36, 36, 38, 36, 36, 34, 36, 54, 38, 56, 44, 42, 44, 58, 60, 62, 48, 4, 6, 8, 8, 10, 46, 64, 14, 26, 28, 26, 46, 22, 22, 36, 26, 38, 40, 38, 42, 36, 36, 46, 38, 66, 42, 42, 44, 46, 46, 46, 48, 38, 12, 41, 39, 50, 50, 46, 48, 22, 24, 26, 52, 25, 23, 21, 54, 36, 54, 38, 40, 13, 54, 11, 9, 46, 7, 5, 3, 1, 68]
SECOND = [-1, -1, -1, -1, 8, -1, -1, 10, -1, -1, -1, 16, 10, -1, -1, -1, -1, -1, -1, -1, -1, 34, -1, -1, 36, -1, -1, 40, -1, -1, 46, -1, -1, 46, 46, 46, 44, 46, 46, -1, 46, 36, 36, 38, 38, -1, 36, 36, 38, 38, 40, 38, 42, 44, 46, 46, -1, 46, -1, 44, 46, 46, -1, -1, -1, 48, 60, 60, 58, 60, 60, 50, -1, 60, 54, 54, 56, 52, 58, 60, 54, 60, 54, 54, 56, 54, 58, 60, 54, 60, -1, 58, 60, 60, 58, 60, 62, 62, 64, 66, 68, 68, 58, 60, 64, 64, 66, 66, 66, 60, 68, 68, 68, 54, 66, 56, 66, 66, 68, 58, 68, 68, 66, 68, 68, 68, 68, -1]


def plan_kernel(plan_ref, table_ref, audio_ref, text_ref, held_ref, pair_ref, code_ref, leaf_ref, sems):
    own = [
        pltpu.make_async_copy(ref, held_ref.at[i], sems.at[i])
        for i, ref in enumerate((audio_ref, text_ref))
    ]
    for copy in own:
        copy.start()
    me = lax.axis_index("dp")
    offsets = [(plan_ref[0, r] - me) & 255 for r in range(ROUNDS)]

    def entry(distance):
        return jnp.maximum(jnp.minimum(distance, 256 - distance) - 1, 0)

    def cost(distance):
        return table_ref[entry(distance)]

    def write(at, transfer, source, target):
        back = transfer & 1
        code_ref[at] = (
            (transfer >> 1)
            | ((2 * source + back) << 8)
            | ((2 * source + 1 - back) << 12)
            | ((2 * target + back) << 16)
            | ((2 * target + 1 - back) << 20)
        )

    far = jnp.int32(1 << 28)
    best = [cost(s) for s in offsets]
    parent = [jnp.int32(0)] * ROUNDS
    away = list(offsets)
    done = [jnp.int32(0)] * ROUNDS
    count = jnp.int32(0)
    for step in range(ROUNDS):
        keys = [jnp.where(done[j] == 1, far, best[j]) for j in range(ROUNDS)]
        first = (keys[0] <= keys[1]) & (keys[0] <= keys[2])
        pick = jnp.where(first, 0, jnp.where(keys[1] <= keys[2], 1, 2))

        def chosen(values):
            return jnp.where(pick == 0, values[0], jnp.where(pick == 1, values[1], values[2]))

        distance = chosen(away)
        at = chosen(offsets)
        mirrored = jnp.where(distance <= HALF, 0, 1)
        one = table_ref[HALF + entry(distance)]
        two = table_ref[2 * HALF + entry(distance)]
        write(count, one ^ mirrored, chosen(parent), step + 1)
        write(count + 1, jnp.maximum(two, 0) ^ mirrored, jnp.int32(step + 1), step + 1)
        count = count + jnp.where(two >= 0, 2, 1)
        for j in range(ROUNDS):
            done[j] = jnp.where(pick == j, 1, done[j])
            onward = (offsets[j] - at) & 255
            price = cost(onward)
            nearer = price < best[j]
            best[j] = jnp.where(nearer, price, best[j])
            parent[j] = jnp.where(nearer, step + 1, parent[j])
            away[j] = jnp.where(nearer, onward, away[j])
    code_ref[count] = -1
    code_ref[7] = -1
    code = code_ref[0]
    leaf_ref[0] = code & 255
    backwards = ((code >> 8) & 1) == 1
    audio, text = audio_ref[...], text_ref[...]
    pair_ref[0] = jnp.where(backwards, text, audio)
    pair_ref[1] = jnp.where(backwards, audio, text)
    for copy in own:
        copy.wait()


def plan_transfers(audio, text, plan):
    smem = pl.BlockSpec(memory_space=pltpu.SMEM)
    vmem = pl.BlockSpec(memory_space=pltpu.VMEM)
    return pl.pallas_call(
        plan_kernel,
        out_shape=(
            jax.ShapeDtypeStruct((2 * (ROUNDS + 1),) + audio.shape, audio.dtype),
            jax.ShapeDtypeStruct((2,) + audio.shape, audio.dtype),
            jax.ShapeDtypeStruct((8,), jnp.int32),
            jax.ShapeDtypeStruct((1,), jnp.int32),
        ),
        in_specs=[smem, smem, vmem, vmem],
        out_specs=(pl.BlockSpec(memory_space=pl.ANY), vmem, smem, smem),
        scratch_shapes=[pltpu.SemaphoreType.DMA((2,))],
        compiler_params=pltpu.CompilerParams(vmem_limit_bytes=16 * MIB),
    )(plan, jnp.asarray(np.array(COST + FIRST + SECOND, np.int32)), audio, text)


def store_kernel(held_in, landed_ref, code_in, held_ref, pair_ref, code_ref, leaf_ref, sems):
    codes = [code_in[i] for i in range(8)]
    targets = [(codes[0] >> 16) & 7, (codes[0] >> 20) & 7]
    stores = [
        pltpu.make_async_copy(landed_ref.at[i], held_ref.at[targets[i]], sems.at[i])
        for i in range(2)
    ]
    for copy in stores:
        copy.start()
    for i in range(7):
        code_ref[i] = codes[i + 1]
    code_ref[7] = -1
    leaf_ref[0] = jnp.where(codes[1] < 0, -1, codes[1] & 255)
    sources = [(codes[1] >> 8) & 7, (codes[1] >> 12) & 7]
    fresh = (sources[0] >> 1) == (targets[0] >> 1)

    @pl.when(fresh)
    def _():
        same = sources[0] == targets[0]
        first, second = landed_ref[0], landed_ref[1]
        pair_ref[0] = jnp.where(same, first, second)
        pair_ref[1] = jnp.where(same, second, first)

    @pl.when(jnp.logical_not(fresh) & (codes[1] >= 0))
    def _():
        loads = [
            pltpu.make_async_copy(held_ref.at[sources[i]], pair_ref.at[i], sems.at[2 + i])
            for i in range(2)
        ]
        for copy in loads:
            copy.start()
        for copy in loads:
            copy.wait()

    for copy in stores:
        copy.wait()


def store_landed(held, landed, codes):
    smem = pl.BlockSpec(memory_space=pltpu.SMEM)
    vmem = pl.BlockSpec(memory_space=pltpu.VMEM)
    return pl.pallas_call(
        store_kernel,
        out_shape=(
            jax.ShapeDtypeStruct(held.shape, held.dtype),
            jax.ShapeDtypeStruct(landed.shape, landed.dtype),
            jax.ShapeDtypeStruct((8,), jnp.int32),
            jax.ShapeDtypeStruct((1,), jnp.int32),
        ),
        in_specs=[pl.BlockSpec(memory_space=pl.ANY), vmem, smem],
        out_specs=(pl.BlockSpec(memory_space=pl.ANY), vmem, smem, smem),
        scratch_shapes=[pltpu.SemaphoreType.DMA((4,))],
        input_output_aliases={0: 0, 2: 2},
        compiler_params=pltpu.CompilerParams(vmem_limit_bytes=16 * MIB),
    )(held, landed, codes)


def swap_kernel(distance, pair_ref, landed_ref, send_sem, recv_sem):
    me = lax.axis_index("dp")
    partners = (lax.rem(me + distance, 256), lax.rem(me + 256 - distance, 256))
    barrier = pltpu.get_barrier_semaphore()
    for device in partners:
        pl.semaphore_signal(barrier, inc=1, device_id=(device,), device_id_type=MESH)
    pl.semaphore_wait(barrier, 2)
    copies = [
        pltpu.make_async_remote_copy(
            src_ref=pair_ref.at[i],
            dst_ref=landed_ref.at[i],
            send_sem=send_sem.at[i],
            recv_sem=recv_sem.at[i],
            device_id=(device,),
            device_id_type=MESH,
        )
        for i, device in enumerate(partners)
    ]
    for copy in copies:
        copy.start()
    for copy in copies:
        copy.wait()


def swap(leaf, pair):
    anywhere = pl.BlockSpec(memory_space=pl.ANY)
    return pl.pallas_call(
        partial(swap_kernel, SHIFTS[leaf]),
        out_shape=jax.ShapeDtypeStruct(pair.shape, pair.dtype),
        in_specs=[anywhere],
        out_specs=anywhere,
        scratch_shapes=[pltpu.SemaphoreType.DMA((2,)), pltpu.SemaphoreType.DMA((2,))],
        compiler_params=pltpu.CompilerParams(
            collective_id=1 + leaf, has_side_effects=True, vmem_limit_bytes=MIB
        ),
    )(pair)


def unit_rows(raw):
    wide = raw.astype(jnp.float32)
    recip = lax.rsqrt(jnp.sum(wide * wide, axis=-1, keepdims=True) + EPSILON)
    wide = wide * recip
    return wide, recip, wide.astype(jnp.bfloat16)


def dot_t(a, b):
    return lax.dot_general(a, b, (((1,), (1,)), ((), ())), preferred_element_type=jnp.float32)


def project(wide, recip, grad):
    along = jnp.sum(wide * grad, axis=-1, keepdims=True)
    return recip * (grad - wide * along)


def loss_kernel(scale_ref, bias_ref, held_ref, row_ref, ga_ref, gt_ref, tot_ref):
    scale = jnp.exp(jnp.full((1, 1), scale_ref[0], jnp.float32))
    bias = bias_ref[0]
    n = held_ref.shape[1]
    rows = lax.broadcasted_iota(jnp.int32, (n, n), 0)
    cols = lax.broadcasted_iota(jnp.int32, (n, n), 1)
    eye = (rows == cols).astype(jnp.float32)

    audio_wide, audio_recip, audio_unit = unit_rows(held_ref[0])
    text_wide, text_recip, text_unit = unit_rows(held_ref[1])
    losses_sum = jnp.zeros((n, n), jnp.float32)
    slopes_sum = jnp.zeros((n, n), jnp.float32)
    scaled_sum = jnp.zeros((n, n), jnp.float32)
    audio_grad = jnp.zeros(audio_wide.shape, jnp.float32)
    text_grad = jnp.zeros(text_wide.shape, jnp.float32)
    for slot in range(ROUNDS + 1):
        far_text = text_unit if slot == 0 else unit_rows(held_ref[2 * slot + 1])[2]
        far_audio = audio_unit if slot == 0 else unit_rows(held_ref[2 * slot])[2]
        scaled = scale * dot_t(audio_unit, far_text)
        logits = scaled + bias
        small = jnp.exp(-jnp.abs(logits))
        slopes = jnp.where(logits >= 0.0, 1.0, small) / (1.0 + small)
        if slot == 0:
            flipped = jnp.where(rows == cols, -logits, logits)
            slopes = slopes - eye
        else:
            flipped = logits
        losses_sum = losses_sum + (jnp.maximum(flipped, 0.0) + jnp.log1p(small))
        slopes_sum = slopes_sum + slopes
        scaled_sum = scaled_sum + slopes * scaled
        weights = (scale * slopes).astype(jnp.bfloat16)
        audio_grad = audio_grad + jnp.dot(weights, far_text, preferred_element_type=jnp.float32)

        logits = scale * dot_t(text_unit, far_audio) + bias
        small = jnp.exp(-jnp.abs(logits))
        slopes = jnp.where(logits >= 0.0, 1.0, small) / (1.0 + small)
        if slot == 0:
            slopes = slopes - eye
        weights = (scale * slopes).astype(jnp.bfloat16)
        text_grad = text_grad + jnp.dot(weights, far_audio, preferred_element_type=jnp.float32)

    ga_ref[...] = project(audio_wide, audio_recip, audio_grad)
    gt_ref[...] = project(text_wide, text_recip, text_grad)
    folded = losses_sum[:, : n // 2] + losses_sum[:, n // 2 :]
    row_ref[...] = jnp.sum(folded.T, axis=0, keepdims=True)
    parts = []
    for total in (losses_sum, slopes_sum, scaled_sum):
        down = jnp.sum(total, axis=0, keepdims=True)
        parts.append(down[:, : n // 2] + down[:, n // 2 :])
    tot_ref[...] = jnp.concatenate(parts + [jnp.zeros((5, n // 2), jnp.float32)], axis=0)


def loss_and_grads(log_scale, bias, held):
    n, d = held.shape[1:]
    vmem = pl.BlockSpec(memory_space=pltpu.VMEM)
    smem = pl.BlockSpec(memory_space=pltpu.SMEM)
    return pl.pallas_call(
        loss_kernel,
        out_shape=(
            jax.ShapeDtypeStruct((1, n), jnp.float32),
            jax.ShapeDtypeStruct((n, d), jnp.float32),
            jax.ShapeDtypeStruct((n, d), jnp.float32),
            jax.ShapeDtypeStruct((8, n // 2), jnp.float32),
        ),
        in_specs=[smem, smem, vmem],
        out_specs=(vmem, vmem, vmem, vmem),
        compiler_params=pltpu.CompilerParams(vmem_limit_bytes=36 * MIB),
    )(log_scale, bias, held)


def stats_kernel(denominator, part_ref, out_ref, *scratch):
    me = lax.axis_index("dp")
    buffers, sends, recvs = scratch[0:3], scratch[3:6], scratch[6:9]
    groups = []
    for stride, peers in STAGES:
        digit = lax.rem(lax.div(me, stride), peers)
        others = []
        for k in range(1, peers):
            other = lax.rem(digit + k, peers)
            others.append((other, me + (other - digit) * stride))
        groups.append((digit, others))
    barrier = pltpu.get_barrier_semaphore()
    count = 0
    for _, others in groups:
        for _, device in others:
            pl.semaphore_signal(barrier, inc=1, device_id=(device,), device_id_type=MESH)
            count += 1
    pl.semaphore_wait(barrier, count)
    value = part_ref[...]
    for stage, (digit, others) in enumerate(groups):
        buffer, send, recv = buffers[stage], sends[stage], recvs[stage]
        buffer[digit] = value
        for other, device in others:
            pltpu.make_async_remote_copy(
                src_ref=buffer.at[digit],
                dst_ref=buffer.at[digit],
                send_sem=send.at[other],
                recv_sem=recv.at[digit],
                device_id=(device,),
                device_id_type=MESH,
            ).start()
        for other, device in others:
            arrived = pltpu.make_async_remote_copy(
                src_ref=buffer.at[digit],
                dst_ref=buffer.at[other],
                send_sem=send.at[other],
                recv_sem=recv.at[other],
                device_id=(device,),
                device_id_type=MESH,
            )
            arrived.wait_recv()
            arrived.wait_send()
        value = buffer[0]
        for j in range(1, STAGES[stage][1]):
            value = value + buffer[j]
    total = jnp.sum(value, axis=1, keepdims=True) / denominator
    out_ref[...] = jnp.broadcast_to(total, out_ref.shape)


def all_stats(parts, denominator):
    vmem = pl.BlockSpec(memory_space=pltpu.VMEM)
    scratch = [pltpu.VMEM((peers,) + parts.shape, jnp.float32) for _, peers in STAGES]
    scratch += [pltpu.SemaphoreType.DMA((peers,)) for _, peers in STAGES] * 2
    return pl.pallas_call(
        partial(stats_kernel, denominator),
        out_shape=jax.ShapeDtypeStruct(parts.shape, jnp.float32),
        in_specs=[vmem],
        out_specs=vmem,
        scratch_shapes=scratch,
        compiler_params=pltpu.CompilerParams(
            collective_id=0, has_side_effects=True, vmem_limit_bytes=4 * MIB
        ),
    )(parts)[:3, 0]


def local(audio, text, log_scale, bias, plan):
    n = audio.shape[0]
    player_count = lax.axis_size("dp")
    leaves = [partial(swap, leaf) for leaf in range(len(SHIFTS))]

    def transfer(state):
        held, pair, codes, leaf = state
        return store_landed(held, lax.switch(leaf[0], leaves, pair), codes)

    state = plan_transfers(audio, text, plan)
    held = lax.while_loop(lambda state: state[3][0] >= 0, transfer, state)[0]
    row_loss, grad_audio, grad_text, parts = loss_and_grads(log_scale, bias, held)
    stats = all_stats(parts, float((ROUNDS + 1) * n * n * player_count))
    return (row_loss.reshape(n), grad_audio, grad_text, stats)


def solution(mesh):
    return jax.shard_map(
        local,
        mesh=mesh,
        in_specs=(P("dp", None), P("dp", None), P(), P(), P("dp", None)),
        out_specs=(P("dp"), P("dp", None), P("dp", None), P()),
        check_vma=False,
    )
```

```python
from functools import partial

import jax
import jax.numpy as jnp
import numpy as np
from jax import lax
from jax.experimental import pallas as pl
from jax.experimental.pallas import tpu as pltpu
from jax.sharding import PartitionSpec as P

EPSILON = 1e-06
ROUNDS = 3
HALF = 128
STAGES = ((1, 8), (8, 4), (32, 8))
MESH = pl.DeviceIdType.MESH
MIB = 1024 * 1024
ANY = pl.BlockSpec(memory_space=pl.ANY)
VMEM = pl.BlockSpec(memory_space=pltpu.VMEM)
SMEM = pl.BlockSpec(memory_space=pltpu.SMEM)

SHIFTS = (1, 2, 5, 6, 7, 8, 9, 16, 19, 21, 23, 24, 25, 26, 28, 30, 31, 32, 33, 34, 36, 37, 41, 42, 43, 45, 46, 50, 54, 55, 57, 61, 64, 67, 128)
COST = [159, 206, 365, 412, 260, 213, 212, 209, 248, 407, 454, 426, 424, 422, 421, 322, 408, 409, 338, 427, 324, 402, 261, 196, 229, 214, 373, 299, 372, 213, 216, 170, 228, 269, 427, 317, 302, 383, 381, 379, 313, 327, 345, 504, 348, 348, 458, 393, 425, 323, 443, 429, 474, 330, 325, 366, 329, 384, 443, 426, 338, 383, 386, 282, 398, 439, 388, 487, 472, 494, 493, 491, 483, 497, 515, 537, 518, 518, 521, 536, 525, 492, 543, 543, 535, 500, 495, 478, 498, 496, 551, 555, 508, 495, 498, 451, 510, 550, 558, 598, 584, 597, 611, 579, 595, 609, 627, 660, 630, 630, 659, 653, 736, 604, 668, 663, 710, 612, 607, 592, 594, 595, 643, 716, 620, 588, 541, 382]
FIRST = [0, 2, 0, 2, 4, 6, 8, 10, 12, 0, 2, 6, 6, 6, 8, 14, 9, 7, 16, 7, 18, 3, 20, 22, 24, 26, 0, 28, 1, 30, 32, 34, 36, 38, 0, 40, 42, 6, 8, 10, 44, 46, 48, 0, 50, 52, 20, 22, 22, 54, 24, 26, 20, 56, 58, 22, 60, 26, 26, 30, 62, 30, 32, 64, 34, 34, 66, 34, 34, 6, 8, 10, 34, 34, 34, 26, 34, 34, 22, 30, 22, 34, 26, 30, 22, 34, 34, 22, 34, 26, 30, 32, 34, 30, 32, 34, 36, 38, 34, 40, 42, 27, 25, 23, 44, 46, 48, 56, 50, 52, 56, 58, 52, 54, 56, 58, 54, 56, 58, 11, 9, 7, 5, 60, 62, 3, 1, 68]
SECOND = [-1, -1, 2, 2, -1, -1, -1, -1, -1, 12, 12, 6, 8, 10, 10, -1, 22, 22, -1, 26, -1, 22, -1, -1, -1, -1, 26, -1, 30, -1, -1, -1, -1, -1, 38, -1, -1, 34, 34, 34, -1, -1, -1, 48, -1, -1, 22, 22, 24, -1, 26, 26, 30, -1, -1, 34, -1, 34, 36, 30, -1, 34, 34, -1, 36, 38, -1, 40, 42, 64, 64, 64, 44, 46, 48, 54, 50, 52, 58, 54, 60, 54, 60, 56, 62, 56, 58, 64, 60, 64, 62, 62, 62, 64, 64, 64, 64, 64, 66, 64, 64, 68, 68, 68, 64, 64, 64, 56, 64, 64, 60, 60, 66, 64, 62, 62, 66, 64, 64, 68, 68, 68, 68, 66, 64, 68, 68, -1]

LANDED = 3
SOURCE, BACK, TARGET, LAST = 8, 10, 11, 13


def plan_kernel(
    plan_ref, table_ref, scale_ref, bias_ref, audio_ref, text_ref,
    pair_ref, code_ref, leaf_ref, scalar_ref, own_ref, held_ref, sems,
):
    loads = [
        pltpu.make_async_copy(ref, pair_ref.at[i], sems.at[i])
        for i, ref in enumerate((audio_ref, text_ref))
    ]
    keeps = [
        pltpu.make_async_copy(pair_ref.at[i], own_ref.at[i], sems.at[2 + i]) for i in range(2)
    ]
    for copy in loads:
        copy.start()
    scalar_ref[0:1, :] = jnp.full((1, 128), scale_ref[0], jnp.float32)
    scalar_ref[1:8, :] = jnp.full((7, 128), bias_ref[0], jnp.float32)
    me = lax.axis_index("dp")
    offsets = [(plan_ref[0, r] - me) & 255 for r in range(ROUNDS)]

    def entry(distance):
        return jnp.maximum(jnp.minimum(distance, 256 - distance) - 1, 0)

    def cost(distance):
        return table_ref[entry(distance)]

    def code(transfer, source, target):
        return (
            (transfer >> 1) | (source << SOURCE) | ((transfer & 1) << BACK) | (target << TARGET)
        )

    for load, keep in zip(loads, keeps):
        load.wait()
        keep.start()
    far = jnp.int32(1 << 28)
    best = [cost(s) for s in offsets]
    parent = [jnp.int32(0)] * ROUNDS
    away = list(offsets)
    done = [jnp.int32(0)] * ROUNDS
    count = jnp.int32(0)
    for step in range(ROUNDS):
        keys = [jnp.where(done[j] == 1, far, best[j]) for j in range(ROUNDS)]
        first = (keys[0] <= keys[1]) & (keys[0] <= keys[2])
        pick = jnp.where(first, 0, jnp.where(keys[1] <= keys[2], 1, 2))

        def chosen(values):
            return jnp.where(pick == 0, values[0], jnp.where(pick == 1, values[1], values[2]))

        distance = chosen(away)
        at = chosen(offsets)
        mirrored = jnp.where(distance <= HALF, 0, 1)
        one = table_ref[HALF + entry(distance)] ^ mirrored
        two = table_ref[2 * HALF + entry(distance)]
        twice = two >= 0
        two = jnp.maximum(two, 0) ^ mirrored
        source = chosen(parent)
        if step > 0:
            source = jnp.where(source == step, LANDED, source)
        code_ref[count] = code(one, source, jnp.where(twice, 0, step + 1))
        code_ref[count + 1] = code(two, LANDED, step + 1)
        count = count + jnp.where(twice, 2, 1)
        for j in range(ROUNDS):
            done[j] = jnp.where(pick == j, 1, done[j])
            onward = (offsets[j] - at) & 255
            price = cost(onward)
            nearer = price < best[j]
            best[j] = jnp.where(nearer, price, best[j])
            parent[j] = jnp.where(nearer, step + 1, parent[j])
            away[j] = jnp.where(nearer, onward, away[j])
    code_ref[count - 1] = code_ref[count - 1] | (1 << LAST)
    leaf_ref[0] = code_ref[0] & 255
    for copy in keeps:
        copy.wait()

    @pl.when(((code_ref[0] >> BACK) & 1) == 1)
    def _():
        audio, text = pair_ref[0], pair_ref[1]
        pair_ref[0] = text
        pair_ref[1] = audio


def plan_transfers(audio, text, log_scale, bias, plan):
    return pl.pallas_call(
        plan_kernel,
        out_shape=(
            jax.ShapeDtypeStruct((2,) + audio.shape, audio.dtype),
            jax.ShapeDtypeStruct((8,), jnp.int32),
            jax.ShapeDtypeStruct((1,), jnp.int32),
            jax.ShapeDtypeStruct((8, 128), jnp.float32),
            jax.ShapeDtypeStruct((2,) + audio.shape, audio.dtype),
            jax.ShapeDtypeStruct((2 * (ROUNDS - 1),) + audio.shape, audio.dtype),
        ),
        in_specs=[SMEM, SMEM, SMEM, SMEM, ANY, ANY],
        out_specs=(VMEM, SMEM, SMEM, VMEM, ANY, ANY),
        scratch_shapes=[pltpu.SemaphoreType.DMA((4,))],
    )(plan, jnp.asarray(np.array(COST + FIRST + SECOND, np.int32)), log_scale, bias, audio, text)


def store_kernel(
    held_in, own_in, landed_ref, code_in,
    held_ref, own_ref, pair_ref, code_ref, leaf_ref, sems,
):
    codes = [code_in[i] for i in range(8)]
    back = (codes[0] >> BACK) & 1
    target = (codes[0] >> TARGET) & 3
    slot = jnp.where(target == 2, 1, 0)
    stores = [
        pltpu.make_async_copy(
            landed_ref.at[i], held_ref.at[2 * slot + (back if i == 0 else 1 - back)], sems.at[i]
        )
        for i in range(2)
    ]

    @pl.when(target > 0)
    def _():
        for copy in stores:
            copy.start()

    for i in range(7):
        code_ref[i] = codes[i + 1]
    code_ref[7] = 0
    leaf_ref[0] = (codes[1] & 255) | (((codes[1] >> LAST) & 1) << 8)
    source = (codes[1] >> SOURCE) & 3
    turn = (codes[1] >> BACK) & 1

    def load(first, second):
        loads = [
            pltpu.make_async_copy(ref, pair_ref.at[i], sems.at[2 + i])
            for i, ref in enumerate((first, second))
        ]
        for copy in loads:
            copy.start()
        for copy in loads:
            copy.wait()

    @pl.when(source == LANDED)
    def _():
        same = back == turn
        first, second = landed_ref[0], landed_ref[1]
        pair_ref[0] = jnp.where(same, first, second)
        pair_ref[1] = jnp.where(same, second, first)

    @pl.when(source == 0)
    def _():
        load(own_ref.at[turn], own_ref.at[1 - turn])

    @pl.when((source == 1) | (source == 2))
    def _():
        at = 2 * jnp.where(source == 2, 1, 0)
        load(held_ref.at[at + turn], held_ref.at[at + 1 - turn])

    @pl.when(target > 0)
    def _():
        for copy in stores:
            copy.wait()


def store_landed(held, own, landed, codes):
    return pl.pallas_call(
        store_kernel,
        out_shape=(
            jax.ShapeDtypeStruct(held.shape, held.dtype),
            jax.ShapeDtypeStruct(own.shape, own.dtype),
            jax.ShapeDtypeStruct(landed.shape, landed.dtype),
            jax.ShapeDtypeStruct((8,), jnp.int32),
            jax.ShapeDtypeStruct((1,), jnp.int32),
        ),
        in_specs=[ANY, ANY, VMEM, SMEM],
        out_specs=(ANY, ANY, VMEM, SMEM, SMEM),
        scratch_shapes=[pltpu.SemaphoreType.DMA((4,))],
        input_output_aliases={0: 0, 1: 1, 3: 3},
    )(held, own, landed, codes)


def swap_kernel(distance, pair_ref, landed_ref, send_sem, recv_sem):
    me = lax.axis_index("dp")
    partners = (lax.rem(me + distance, 256), lax.rem(me + 256 - distance, 256))
    barrier = pltpu.get_barrier_semaphore()
    for device in partners:
        pl.semaphore_signal(barrier, inc=1, device_id=(device,), device_id_type=MESH)
    pl.semaphore_wait(barrier, 2)
    copies = [
        pltpu.make_async_remote_copy(
            src_ref=pair_ref.at[i],
            dst_ref=landed_ref.at[i],
            send_sem=send_sem.at[i],
            recv_sem=recv_sem.at[i],
            device_id=(device,),
            device_id_type=MESH,
        )
        for i, device in enumerate(partners)
    ]
    for copy in copies:
        copy.start()
    for copy in copies:
        copy.wait()


def swap(leaf, pair):
    return pl.pallas_call(
        partial(swap_kernel, SHIFTS[leaf]),
        out_shape=jax.ShapeDtypeStruct(pair.shape, pair.dtype),
        in_specs=[ANY],
        out_specs=ANY,
        scratch_shapes=[pltpu.SemaphoreType.DMA((2,)), pltpu.SemaphoreType.DMA((2,))],
        compiler_params=pltpu.CompilerParams(
            collective_id=1 + leaf, has_side_effects=True, vmem_limit_bytes=MIB
        ),
    )(pair)


def unit_rows(raw):
    wide = raw.astype(jnp.float32)
    recip = lax.rsqrt(jnp.sum(wide * wide, axis=-1, keepdims=True) + EPSILON)
    wide = wide * recip
    return wide, recip, wide.astype(jnp.bfloat16)


def dot_t(a, b):
    return lax.dot_general(a, b, (((1,), (1,)), ((), ())), preferred_element_type=jnp.float32)


def project(wide, recip, grad):
    along = jnp.sum(wide * grad, axis=-1, keepdims=True)
    return recip * (grad - wide * along)


def loss_kernel(
    scalar_ref, code_ref, audio_ref, text_ref, held_ref, landed_ref,
    row_ref, ga_ref, gt_ref, tot_ref, audio_out, text_out, sems,
):
    n = audio_ref.shape[0]
    scale = jnp.exp(scalar_ref[0:1, 0:1])
    bias = scalar_ref[1:2, 0:1]
    rows = lax.broadcasted_iota(jnp.int32, (n, n), 0)
    cols = lax.broadcasted_iota(jnp.int32, (n, n), 1)
    eye = (rows == cols).astype(jnp.float32)
    backwards = ((code_ref[0] >> BACK) & 1) == 1

    audio_wide, audio_recip, audio_unit = unit_rows(audio_ref[...])
    text_wide, text_recip, text_unit = unit_rows(text_ref[...])
    losses_sum = jnp.zeros((n, n), jnp.float32)
    slopes_sum = jnp.zeros((n, n), jnp.float32)
    scaled_sum = jnp.zeros((n, n), jnp.float32)
    audio_grad = jnp.zeros(audio_wide.shape, jnp.float32)
    text_grad = jnp.zeros(text_wide.shape, jnp.float32)
    for slot in range(ROUNDS + 1):
        if slot == 0:
            far_text = text_unit
        elif slot < ROUNDS:
            far_text = unit_rows(held_ref[2 * slot - 1])[2]
        else:
            far_text = unit_rows(jnp.where(backwards, landed_ref[0], landed_ref[1]))[2]
        scaled = scale * dot_t(audio_unit, far_text)
        logits = scaled + bias
        small = jnp.exp(-jnp.abs(logits))
        slopes = jnp.where(logits >= 0.0, 1.0, small) / (1.0 + small)
        if slot == 0:
            flipped = jnp.where(rows == cols, -logits, logits)
            slopes = slopes - eye
        else:
            flipped = logits
        losses_sum = losses_sum + (jnp.maximum(flipped, 0.0) + jnp.log1p(small))
        slopes_sum = slopes_sum + slopes
        scaled_sum = scaled_sum + slopes * scaled
        weights = (scale * slopes).astype(jnp.bfloat16)
        audio_grad = audio_grad + jnp.dot(weights, far_text, preferred_element_type=jnp.float32)
    audio_out[...] = project(audio_wide, audio_recip, audio_grad)
    audio_store = pltpu.make_async_copy(audio_out, ga_ref, sems.at[0])
    audio_store.start()

    for slot in range(ROUNDS + 1):
        if slot == 0:
            far_audio = audio_unit
        elif slot < ROUNDS:
            far_audio = unit_rows(held_ref[2 * slot - 2])[2]
        else:
            far_audio = unit_rows(jnp.where(backwards, landed_ref[1], landed_ref[0]))[2]
        logits = scale * dot_t(text_unit, far_audio) + bias
        small = jnp.exp(-jnp.abs(logits))
        slopes = jnp.where(logits >= 0.0, 1.0, small) / (1.0 + small)
        if slot == 0:
            slopes = slopes - eye
        weights = (scale * slopes).astype(jnp.bfloat16)
        text_grad = text_grad + jnp.dot(weights, far_audio, preferred_element_type=jnp.float32)
    text_out[...] = project(text_wide, text_recip, text_grad)
    text_store = pltpu.make_async_copy(text_out, gt_ref, sems.at[1])
    text_store.start()

    folded = losses_sum[:, : n // 2] + losses_sum[:, n // 2 :]
    row_ref[...] = jnp.sum(folded.T, axis=0, keepdims=True)
    parts = []
    for total in (losses_sum, slopes_sum, scaled_sum):
        down = jnp.sum(total, axis=0, keepdims=True)
        parts.append(down[:, : n // 2] + down[:, n // 2 :])
    tot_ref[...] = jnp.concatenate(parts + [jnp.zeros((5, n // 2), jnp.float32)], axis=0)
    audio_store.wait()
    text_store.wait()


def loss_and_grads(scalars, codes, audio, text, held, landed):
    n, d = audio.shape
    return pl.pallas_call(
        loss_kernel,
        out_shape=(
            jax.ShapeDtypeStruct((1, n), jnp.float32),
            jax.ShapeDtypeStruct((n, d), jnp.float32),
            jax.ShapeDtypeStruct((n, d), jnp.float32),
            jax.ShapeDtypeStruct((8, n // 2), jnp.float32),
        ),
        in_specs=[VMEM, SMEM, VMEM, VMEM, VMEM, VMEM],
        out_specs=(VMEM, ANY, ANY, VMEM),
        scratch_shapes=[
            pltpu.VMEM((n, d), jnp.float32),
            pltpu.VMEM((n, d), jnp.float32),
            pltpu.SemaphoreType.DMA((2,)),
        ],
        compiler_params=pltpu.CompilerParams(vmem_limit_bytes=40 * MIB),
    )(scalars, codes, audio, text, held, landed)


def stats_kernel(denominator, part_ref, out_ref, *scratch):
    me = lax.axis_index("dp")
    buffers, sends, recvs = scratch[0:3], scratch[3:6], scratch[6:9]
    groups = []
    for stride, peers in STAGES:
        digit = lax.rem(lax.div(me, stride), peers)
        others = []
        for k in range(1, peers):
            other = lax.rem(digit + k, peers)
            others.append((other, me + (other - digit) * stride))
        groups.append((digit, others))
    barrier = pltpu.get_barrier_semaphore()
    count = 0
    for _, others in groups:
        for _, device in others:
            pl.semaphore_signal(barrier, inc=1, device_id=(device,), device_id_type=MESH)
            count += 1
    pl.semaphore_wait(barrier, count)
    value = part_ref[...]
    sent = []
    for stage, (digit, others) in enumerate(groups):
        buffer, send, recv = buffers[stage], sends[stage], recvs[stage]
        buffer[digit] = value
        for other, device in others:
            pltpu.make_async_remote_copy(
                src_ref=buffer.at[digit],
                dst_ref=buffer.at[digit],
                send_sem=send.at[other],
                recv_sem=recv.at[digit],
                device_id=(device,),
                device_id_type=MESH,
            ).start()
        for other, device in others:
            arrived = pltpu.make_async_remote_copy(
                src_ref=buffer.at[digit],
                dst_ref=buffer.at[other],
                send_sem=send.at[other],
                recv_sem=recv.at[other],
                device_id=(device,),
                device_id_type=MESH,
            )
            arrived.wait_recv()
            sent.append(arrived)
        value = buffer[0]
        for j in range(1, STAGES[stage][1]):
            value = value + buffer[j]
    for copy in sent:
        copy.wait_send()
    total = jnp.sum(value, axis=1, keepdims=True) / denominator
    out_ref[...] = jnp.broadcast_to(total, out_ref.shape)


def all_stats(parts, denominator):
    scratch = [pltpu.VMEM((peers,) + parts.shape, jnp.float32) for _, peers in STAGES]
    scratch += [pltpu.SemaphoreType.DMA((peers,)) for _, peers in STAGES] * 2
    return pl.pallas_call(
        partial(stats_kernel, denominator),
        out_shape=jax.ShapeDtypeStruct(parts.shape, jnp.float32),
        in_specs=[VMEM],
        out_specs=VMEM,
        scratch_shapes=scratch,
        compiler_params=pltpu.CompilerParams(
            collective_id=0, has_side_effects=True, vmem_limit_bytes=4 * MIB
        ),
    )(parts)[:3, 0]


def local(audio, text, log_scale, bias, plan):
    n, d = audio.shape
    player_count = lax.axis_size("dp")
    leaves = [partial(swap, leaf) for leaf in range(len(SHIFTS))]
    pair, codes, leaf, scalars, own, held = plan_transfers(audio, text, log_scale, bias, plan)

    def transfer(state):
        held, own, pair, codes, leaf = state
        landed = lax.switch(leaf[0], leaves, pair)
        return store_landed(held, own, landed, codes)

    state = (held, own, pair, codes, leaf)
    held, _, pair, codes, leaf = lax.while_loop(lambda s: s[4][0] < 256, transfer, state)
    landed = lax.switch(leaf[0] - 256, leaves, pair)
    row_loss, grad_audio, grad_text, parts = loss_and_grads(
        scalars, codes, audio, text, held, landed
    )
    stats = all_stats(parts, float((ROUNDS + 1) * n * n * player_count))
    return (row_loss.reshape(n), grad_audio, grad_text, stats)


def solution(mesh):
    return jax.shard_map(
        local,
        mesh=mesh,
        in_specs=(P("dp", None), P("dp", None), P(), P(), P("dp", None)),
        out_specs=(P("dp"), P("dp", None), P("dp", None), P()),
        check_vma=False,
    )
```

```python
from functools import partial

import jax
import jax.numpy as jnp
import numpy as np
from jax import lax
from jax.experimental import pallas as pl
from jax.experimental.pallas import tpu as pltpu
from jax.sharding import PartitionSpec as P

EPSILON = 1e-06
ROUNDS = 3
HALF = 128
STAGES = ((1, 8), (8, 4), (32, 8))
MESH = pl.DeviceIdType.MESH
MIB = 1024 * 1024
ANY = pl.BlockSpec(memory_space=pl.ANY)
VMEM = pl.BlockSpec(memory_space=pltpu.VMEM)
SMEM = pl.BlockSpec(memory_space=pltpu.SMEM)

SHIFTS = (1, 2, 5, 6, 7, 8, 9, 16, 19, 21, 23, 24, 25, 26, 28, 30, 31, 32, 33, 34, 36, 37, 41, 42, 43, 45, 46, 50, 54, 55, 57, 61, 64, 67, 128)
COST = [159, 206, 365, 412, 260, 213, 212, 209, 248, 407, 454, 426, 424, 422, 421, 322, 408, 409, 338, 427, 324, 402, 261, 196, 229, 214, 373, 299, 372, 213, 216, 170, 228, 269, 427, 317, 302, 383, 381, 379, 313, 327, 345, 504, 348, 348, 458, 393, 425, 323, 443, 429, 474, 330, 325, 366, 329, 384, 443, 426, 338, 383, 386, 282, 398, 439, 388, 487, 472, 494, 493, 491, 483, 497, 515, 537, 518, 518, 521, 536, 525, 492, 543, 543, 535, 500, 495, 478, 498, 496, 551, 555, 508, 495, 498, 451, 510, 550, 558, 598, 584, 597, 611, 579, 595, 609, 627, 660, 630, 630, 659, 653, 736, 604, 668, 663, 710, 612, 607, 592, 594, 595, 643, 716, 620, 588, 541, 382]
FIRST = [0, 2, 0, 2, 4, 6, 8, 10, 12, 0, 2, 6, 6, 6, 8, 14, 9, 7, 16, 7, 18, 3, 20, 22, 24, 26, 0, 28, 1, 30, 32, 34, 36, 38, 0, 40, 42, 6, 8, 10, 44, 46, 48, 0, 50, 52, 20, 22, 22, 54, 24, 26, 20, 56, 58, 22, 60, 26, 26, 30, 62, 30, 32, 64, 34, 34, 66, 34, 34, 6, 8, 10, 34, 34, 34, 26, 34, 34, 22, 30, 22, 34, 26, 30, 22, 34, 34, 22, 34, 26, 30, 32, 34, 30, 32, 34, 36, 38, 34, 40, 42, 27, 25, 23, 44, 46, 48, 56, 50, 52, 56, 58, 52, 54, 56, 58, 54, 56, 58, 11, 9, 7, 5, 60, 62, 3, 1, 68]
SECOND = [-1, -1, 2, 2, -1, -1, -1, -1, -1, 12, 12, 6, 8, 10, 10, -1, 22, 22, -1, 26, -1, 22, -1, -1, -1, -1, 26, -1, 30, -1, -1, -1, -1, -1, 38, -1, -1, 34, 34, 34, -1, -1, -1, 48, -1, -1, 22, 22, 24, -1, 26, 26, 30, -1, -1, 34, -1, 34, 36, 30, -1, 34, 34, -1, 36, 38, -1, 40, 42, 64, 64, 64, 44, 46, 48, 54, 50, 52, 58, 54, 60, 54, 60, 56, 62, 56, 58, 64, 60, 64, 62, 62, 62, 64, 64, 64, 64, 64, 66, 64, 64, 68, 68, 68, 64, 64, 64, 56, 64, 64, 60, 60, 66, 64, 62, 62, 66, 64, 64, 68, 68, 68, 68, 66, 64, 68, 68, -1]

LANDED = 3
SOURCE, BACK, TARGET, LAST = 8, 10, 11, 13


def plan_kernel(
    plan_ref, table_ref, scale_ref, bias_ref, audio_ref, text_ref,
    pair_ref, code_ref, leaf_ref, scalar_ref, own_ref, held_ref, sems,
):
    loads = [
        pltpu.make_async_copy(ref, pair_ref.at[i], sems.at[i])
        for i, ref in enumerate((audio_ref, text_ref))
    ]
    keeps = [
        pltpu.make_async_copy(pair_ref.at[i], own_ref.at[i], sems.at[2 + i]) for i in range(2)
    ]
    for copy in loads:
        copy.start()
    scalar_ref[0:1, :] = jnp.full((1, 128), scale_ref[0], jnp.float32)
    scalar_ref[1:8, :] = jnp.full((7, 128), bias_ref[0], jnp.float32)
    me = lax.axis_index("dp")
    offsets = [(plan_ref[0, r] - me) & 255 for r in range(ROUNDS)]

    def entry(distance):
        return jnp.maximum(jnp.minimum(distance, 256 - distance) - 1, 0)

    def cost(distance):
        return table_ref[entry(distance)]

    def code(transfer, source, target):
        return (
            (transfer >> 1) | (source << SOURCE) | ((transfer & 1) << BACK) | (target << TARGET)
        )

    for load, keep in zip(loads, keeps):
        load.wait()
        keep.start()
    far = jnp.int32(1 << 28)
    best = [cost(s) for s in offsets]
    parent = [jnp.int32(0)] * ROUNDS
    away = list(offsets)
    done = [jnp.int32(0)] * ROUNDS
    count = jnp.int32(0)
    for step in range(ROUNDS):
        keys = [jnp.where(done[j] == 1, far, best[j]) for j in range(ROUNDS)]
        first = (keys[0] <= keys[1]) & (keys[0] <= keys[2])
        pick = jnp.where(first, 0, jnp.where(keys[1] <= keys[2], 1, 2))

        def chosen(values):
            return jnp.where(pick == 0, values[0], jnp.where(pick == 1, values[1], values[2]))

        distance = chosen(away)
        at = chosen(offsets)
        mirrored = jnp.where(distance <= HALF, 0, 1)
        one = table_ref[HALF + entry(distance)] ^ mirrored
        two = table_ref[2 * HALF + entry(distance)]
        twice = two >= 0
        two = jnp.maximum(two, 0) ^ mirrored
        source = chosen(parent)
        if step > 0:
            source = jnp.where(source == step, LANDED, source)
        code_ref[count] = code(one, source, jnp.where(twice, 0, step + 1))
        code_ref[count + 1] = code(two, LANDED, step + 1)
        count = count + jnp.where(twice, 2, 1)
        for j in range(ROUNDS):
            done[j] = jnp.where(pick == j, 1, done[j])
            onward = (offsets[j] - at) & 255
            price = cost(onward)
            nearer = price < best[j]
            best[j] = jnp.where(nearer, price, best[j])
            parent[j] = jnp.where(nearer, step + 1, parent[j])
            away[j] = jnp.where(nearer, onward, away[j])
    code_ref[count - 1] = code_ref[count - 1] | (1 << LAST)
    leaf_ref[0] = code_ref[0] & 255
    for copy in keeps:
        copy.wait()

    @pl.when(((code_ref[0] >> BACK) & 1) == 1)
    def _():
        audio, text = pair_ref[0], pair_ref[1]
        pair_ref[0] = text
        pair_ref[1] = audio


def plan_transfers(audio, text, log_scale, bias, plan):
    return pl.pallas_call(
        plan_kernel,
        out_shape=(
            jax.ShapeDtypeStruct((2,) + audio.shape, audio.dtype),
            jax.ShapeDtypeStruct((8,), jnp.int32),
            jax.ShapeDtypeStruct((1,), jnp.int32),
            jax.ShapeDtypeStruct((8, 128), jnp.float32),
            jax.ShapeDtypeStruct((2,) + audio.shape, audio.dtype),
            jax.ShapeDtypeStruct((2 * (ROUNDS - 1),) + audio.shape, audio.dtype),
        ),
        in_specs=[SMEM, SMEM, SMEM, SMEM, ANY, ANY],
        out_specs=(VMEM, SMEM, SMEM, VMEM, ANY, ANY),
        scratch_shapes=[pltpu.SemaphoreType.DMA((4,))],
    )(plan, jnp.asarray(np.array(COST + FIRST + SECOND, np.int32)), log_scale, bias, audio, text)


def store_kernel(
    held_in, own_in, landed_ref, code_in,
    held_ref, own_ref, pair_ref, code_ref, leaf_ref, sems,
):
    codes = [code_in[i] for i in range(8)]
    back = (codes[0] >> BACK) & 1
    target = (codes[0] >> TARGET) & 3
    slot = jnp.where(target == 2, 1, 0)
    stores = [
        pltpu.make_async_copy(
            landed_ref.at[i], held_ref.at[2 * slot + (back if i == 0 else 1 - back)], sems.at[i]
        )
        for i in range(2)
    ]

    @pl.when(target > 0)
    def _():
        for copy in stores:
            copy.start()

    for i in range(7):
        code_ref[i] = codes[i + 1]
    code_ref[7] = 0
    leaf_ref[0] = (codes[1] & 255) | (((codes[1] >> LAST) & 1) << 8)
    source = (codes[1] >> SOURCE) & 3
    turn = (codes[1] >> BACK) & 1

    def load(first, second):
        loads = [
            pltpu.make_async_copy(ref, pair_ref.at[i], sems.at[2 + i])
            for i, ref in enumerate((first, second))
        ]
        for copy in loads:
            copy.start()
        for copy in loads:
            copy.wait()

    @pl.when(source == LANDED)
    def _():
        same = back == turn
        first, second = landed_ref[0], landed_ref[1]
        pair_ref[0] = jnp.where(same, first, second)
        pair_ref[1] = jnp.where(same, second, first)

    @pl.when(source == 0)
    def _():
        load(own_ref.at[turn], own_ref.at[1 - turn])

    @pl.when((source == 1) | (source == 2))
    def _():
        at = 2 * jnp.where(source == 2, 1, 0)
        load(held_ref.at[at + turn], held_ref.at[at + 1 - turn])

    @pl.when(target > 0)
    def _():
        for copy in stores:
            copy.wait()


def store_landed(held, own, landed, codes):
    return pl.pallas_call(
        store_kernel,
        out_shape=(
            jax.ShapeDtypeStruct(held.shape, held.dtype),
            jax.ShapeDtypeStruct(own.shape, own.dtype),
            jax.ShapeDtypeStruct(landed.shape, landed.dtype),
            jax.ShapeDtypeStruct((8,), jnp.int32),
            jax.ShapeDtypeStruct((1,), jnp.int32),
        ),
        in_specs=[ANY, ANY, VMEM, SMEM],
        out_specs=(ANY, ANY, VMEM, SMEM, SMEM),
        scratch_shapes=[pltpu.SemaphoreType.DMA((4,))],
        input_output_aliases={0: 0, 1: 1, 3: 3},
    )(held, own, landed, codes)


def swap_kernel(distance, pair_ref, landed_ref, send_sem, recv_sem):
    me = lax.axis_index("dp")
    partners = (lax.rem(me + distance, 256), lax.rem(me + 256 - distance, 256))
    barrier = pltpu.get_barrier_semaphore()
    for device in partners:
        pl.semaphore_signal(barrier, inc=1, device_id=(device,), device_id_type=MESH)
    pl.semaphore_wait(barrier, 2)
    copies = [
        pltpu.make_async_remote_copy(
            src_ref=pair_ref.at[i],
            dst_ref=landed_ref.at[i],
            send_sem=send_sem.at[i],
            recv_sem=recv_sem.at[i],
            device_id=(device,),
            device_id_type=MESH,
        )
        for i, device in enumerate(partners)
    ]
    for copy in copies:
        copy.start()
    for copy in copies:
        copy.wait()


def swap(leaf, pair):
    return pl.pallas_call(
        partial(swap_kernel, SHIFTS[leaf]),
        out_shape=jax.ShapeDtypeStruct(pair.shape, pair.dtype),
        in_specs=[ANY],
        out_specs=ANY,
        scratch_shapes=[pltpu.SemaphoreType.DMA((2,)), pltpu.SemaphoreType.DMA((2,))],
        compiler_params=pltpu.CompilerParams(
            collective_id=1 + leaf, has_side_effects=True, vmem_limit_bytes=MIB
        ),
    )(pair)


def unit_rows(raw):
    wide = raw.astype(jnp.float32)
    recip = lax.rsqrt(jnp.sum(wide * wide, axis=-1, keepdims=True) + EPSILON)
    wide = wide * recip
    return wide, recip, wide.astype(jnp.bfloat16)


def dot_t(a, b):
    return lax.dot_general(a, b, (((1,), (1,)), ((), ())), preferred_element_type=jnp.float32)


def project(wide, recip, grad):
    along = jnp.sum(wide * grad, axis=-1, keepdims=True)
    return recip * (grad - wide * along)


def loss_kernel(
    denominator, scalar_ref, code_ref, audio_ref, text_ref, held_ref, landed_ref,
    row_ref, ga_ref, gt_ref, stats_ref, audio_out, text_out, sems, *scratch,
):
    me = lax.axis_index("dp")
    count = len(STAGES)
    buffers, sends, recvs = [scratch[i * count : (i + 1) * count] for i in range(3)]
    groups = []
    for stride, peers in STAGES:
        digit = lax.rem(lax.div(me, stride), peers)
        others = []
        for k in range(1, peers):
            other = lax.rem(digit + k, peers)
            others.append((other, me + (other - digit) * stride))
        groups.append((digit, others))
    barrier = pltpu.get_barrier_semaphore()
    for _, others in groups:
        for _, device in others:
            pl.semaphore_signal(barrier, inc=1, device_id=(device,), device_id_type=MESH)

    def copies(stage):
        digit, others = groups[stage]
        return [
            pltpu.make_async_remote_copy(
                src_ref=buffers[stage].at[digit],
                dst_ref=buffers[stage].at[digit],
                send_sem=sends[stage].at[other],
                recv_sem=recvs[stage].at[digit],
                device_id=(device,),
                device_id_type=MESH,
            )
            for other, device in others
        ]

    def send(stage, value):
        buffers[stage][groups[stage][0]] = value
        for copy in copies(stage):
            copy.start()

    def receive(stage):
        digit, others = groups[stage]
        for other, device in others:
            pltpu.make_async_remote_copy(
                src_ref=buffers[stage].at[digit],
                dst_ref=buffers[stage].at[other],
                send_sem=sends[stage].at[other],
                recv_sem=recvs[stage].at[other],
                device_id=(device,),
                device_id_type=MESH,
            ).wait_recv()
        value = buffers[stage][0]
        for j in range(1, STAGES[stage][1]):
            value = value + buffers[stage][j]
        return value

    n = audio_ref.shape[0]
    scale = jnp.exp(scalar_ref[0:1, 0:1])
    bias = scalar_ref[1:2, 0:1]
    rows = lax.broadcasted_iota(jnp.int32, (n, n), 0)
    cols = lax.broadcasted_iota(jnp.int32, (n, n), 1)
    eye = (rows == cols).astype(jnp.float32)
    backwards = ((code_ref[0] >> BACK) & 1) == 1
    audio_wide, audio_recip, audio_unit = unit_rows(audio_ref[...])
    text_wide, text_recip, text_unit = unit_rows(text_ref[...])
    losses_sum = jnp.zeros((n, n), jnp.float32)
    slopes_sum = jnp.zeros((n, n), jnp.float32)
    scaled_sum = jnp.zeros((n, n), jnp.float32)
    far_texts, far_weights = [], []
    for slot in range(ROUNDS + 1):
        if slot == 0:
            far_text = text_unit
        elif slot < ROUNDS:
            far_text = unit_rows(held_ref[2 * slot - 1])[2]
        else:
            far_text = unit_rows(jnp.where(backwards, landed_ref[0], landed_ref[1]))[2]
        scaled = scale * dot_t(audio_unit, far_text)
        logits = scaled + bias
        small = jnp.exp(-jnp.abs(logits))
        slopes = jnp.where(logits >= 0.0, 1.0, small) / (1.0 + small)
        if slot == 0:
            flipped = jnp.where(rows == cols, -logits, logits)
            slopes = slopes - eye
        else:
            flipped = logits
        losses_sum = losses_sum + (jnp.maximum(flipped, 0.0) + jnp.log1p(small))
        slopes_sum = slopes_sum + slopes
        scaled_sum = scaled_sum + slopes * scaled
        far_texts.append(far_text)
        far_weights.append((scale * slopes).astype(jnp.bfloat16))

    parts = []
    for total in (losses_sum, slopes_sum, scaled_sum):
        down = jnp.sum(total, axis=0, keepdims=True)
        parts.append(down[:, : n // 2] + down[:, n // 2 :])
    parts = jnp.concatenate(parts + [jnp.zeros((5, n // 2), jnp.float32)], axis=0)
    pl.semaphore_wait(barrier, sum(peers - 1 for _, peers in STAGES))
    send(0, parts)

    audio_grad = jnp.zeros(audio_wide.shape, jnp.float32)
    for far_text, weights in zip(far_texts, far_weights):
        audio_grad = audio_grad + jnp.dot(weights, far_text, preferred_element_type=jnp.float32)
    audio_out[...] = project(audio_wide, audio_recip, audio_grad)
    audio_store = pltpu.make_async_copy(audio_out, ga_ref, sems.at[0])
    audio_store.start()
    send(1, receive(0))

    text_grad = jnp.zeros(text_wide.shape, jnp.float32)
    for slot in range(ROUNDS + 1):
        if slot == 0:
            far_audio = audio_unit
        elif slot < ROUNDS:
            far_audio = unit_rows(held_ref[2 * slot - 2])[2]
        else:
            far_audio = unit_rows(jnp.where(backwards, landed_ref[1], landed_ref[0]))[2]
        logits = scale * dot_t(text_unit, far_audio) + bias
        small = jnp.exp(-jnp.abs(logits))
        slopes = jnp.where(logits >= 0.0, 1.0, small) / (1.0 + small)
        if slot == 0:
            slopes = slopes - eye
        weights = (scale * slopes).astype(jnp.bfloat16)
        text_grad = text_grad + jnp.dot(weights, far_audio, preferred_element_type=jnp.float32)
        if slot == 1:
            send(2, receive(1))
    text_out[...] = project(text_wide, text_recip, text_grad)
    text_store = pltpu.make_async_copy(text_out, gt_ref, sems.at[1])
    text_store.start()
    folded = losses_sum[:, : n // 2] + losses_sum[:, n // 2 :]
    row_ref[...] = jnp.sum(folded.T, axis=0, keepdims=True)
    total = jnp.sum(receive(2), axis=1, keepdims=True) / denominator
    stats_ref[...] = jnp.broadcast_to(total, stats_ref.shape)
    for stage in range(len(STAGES)):
        for copy in copies(stage):
            copy.wait_send()
    audio_store.wait()
    text_store.wait()


def loss_and_grads(denominator, scalars, codes, audio, text, held, landed):
    n, d = audio.shape
    part = (8, n // 2)
    return pl.pallas_call(
        partial(loss_kernel, denominator),
        out_shape=(
            jax.ShapeDtypeStruct((1, n), jnp.float32),
            jax.ShapeDtypeStruct((n, d), jnp.float32),
            jax.ShapeDtypeStruct((n, d), jnp.float32),
            jax.ShapeDtypeStruct(part, jnp.float32),
        ),
        in_specs=[VMEM, SMEM, VMEM, VMEM, VMEM, VMEM],
        out_specs=(VMEM, ANY, ANY, VMEM),
        scratch_shapes=[
            pltpu.VMEM((n, d), jnp.float32),
            pltpu.VMEM((n, d), jnp.float32),
            pltpu.SemaphoreType.DMA((2,)),
        ]
        + [pltpu.VMEM((peers,) + part, jnp.float32) for _, peers in STAGES]
        + [pltpu.SemaphoreType.DMA((peers,)) for _, peers in STAGES] * 2,
        compiler_params=pltpu.CompilerParams(
            collective_id=0, has_side_effects=True, vmem_limit_bytes=40 * MIB
        ),
    )(scalars, codes, audio, text, held, landed)


def local(audio, text, log_scale, bias, plan):
    n, d = audio.shape
    player_count = lax.axis_size("dp")
    leaves = [partial(swap, leaf) for leaf in range(len(SHIFTS))]
    pair, codes, leaf, scalars, own, held = plan_transfers(audio, text, log_scale, bias, plan)

    def transfer(state):
        held, own, pair, codes, leaf = state
        landed = lax.switch(leaf[0], leaves, pair)
        return store_landed(held, own, landed, codes)

    state = (held, own, pair, codes, leaf)
    held, _, pair, codes, leaf = lax.while_loop(lambda s: s[4][0] < 256, transfer, state)
    landed = lax.switch(leaf[0] - 256, leaves, pair)
    row_loss, grad_audio, grad_text, stats = loss_and_grads(
        float((ROUNDS + 1) * n * n * player_count), scalars, codes, audio, text, held, landed
    )
    return (row_loss.reshape(n), grad_audio, grad_text, stats[:3, 0])


def solution(mesh):
    return jax.shard_map(
        local,
        mesh=mesh,
        in_specs=(P("dp", None), P("dp", None), P(), P(), P("dp", None)),
        out_specs=(P("dp"), P("dp", None), P("dp", None), P()),
        check_vma=False,
    )
```

```python
from functools import partial

import jax
import jax.numpy as jnp
import numpy as np
from jax import lax
from jax.experimental import pallas as pl
from jax.experimental.pallas import tpu as pltpu
from jax.sharding import PartitionSpec as P

EPSILON = 1e-06
ROUNDS = 3
HALF = 128
STAGES = ((1, 8), (8, 4), (32, 8))
MESH = pl.DeviceIdType.MESH
MIB = 1024 * 1024
ANY = pl.BlockSpec(memory_space=pl.ANY)
VMEM = pl.BlockSpec(memory_space=pltpu.VMEM)
SMEM = pl.BlockSpec(memory_space=pltpu.SMEM)

SHIFTS = (1, 2, 5, 6, 7, 8, 9, 16, 19, 21, 23, 24, 25, 26, 28, 30, 31, 32, 33, 34, 36, 37, 41, 42, 43, 45, 46, 50, 54, 55, 57, 61, 64, 67, 128)
COST = [159, 206, 365, 412, 260, 213, 212, 209, 248, 407, 454, 426, 424, 422, 421, 322, 408, 409, 338, 427, 324, 402, 261, 196, 229, 214, 373, 299, 372, 213, 216, 170, 228, 269, 427, 317, 302, 383, 381, 379, 313, 327, 345, 504, 348, 348, 458, 393, 425, 323, 443, 429, 474, 330, 325, 366, 329, 384, 443, 426, 338, 383, 386, 282, 398, 439, 388, 487, 472, 494, 493, 491, 483, 497, 515, 537, 518, 518, 521, 536, 525, 492, 543, 543, 535, 500, 495, 478, 498, 496, 551, 555, 508, 495, 498, 451, 510, 550, 558, 598, 584, 597, 611, 579, 595, 609, 627, 660, 630, 630, 659, 653, 736, 604, 668, 663, 710, 612, 607, 592, 594, 595, 643, 716, 620, 588, 541, 382]
FIRST = [0, 2, 0, 2, 4, 6, 8, 10, 12, 0, 2, 6, 6, 6, 8, 14, 9, 7, 16, 7, 18, 3, 20, 22, 24, 26, 0, 28, 1, 30, 32, 34, 36, 38, 0, 40, 42, 6, 8, 10, 44, 46, 48, 0, 50, 52, 20, 22, 22, 54, 24, 26, 20, 56, 58, 22, 60, 26, 26, 30, 62, 30, 32, 64, 34, 34, 66, 34, 34, 6, 8, 10, 34, 34, 34, 26, 34, 34, 22, 30, 22, 34, 26, 30, 22, 34, 34, 22, 34, 26, 30, 32, 34, 30, 32, 34, 36, 38, 34, 40, 42, 27, 25, 23, 44, 46, 48, 56, 50, 52, 56, 58, 52, 54, 56, 58, 54, 56, 58, 11, 9, 7, 5, 60, 62, 3, 1, 68]
SECOND = [-1, -1, 2, 2, -1, -1, -1, -1, -1, 12, 12, 6, 8, 10, 10, -1, 22, 22, -1, 26, -1, 22, -1, -1, -1, -1, 26, -1, 30, -1, -1, -1, -1, -1, 38, -1, -1, 34, 34, 34, -1, -1, -1, 48, -1, -1, 22, 22, 24, -1, 26, 26, 30, -1, -1, 34, -1, 34, 36, 30, -1, 34, 34, -1, 36, 38, -1, 40, 42, 64, 64, 64, 44, 46, 48, 54, 50, 52, 58, 54, 60, 54, 60, 56, 62, 56, 58, 64, 60, 64, 62, 62, 62, 64, 64, 64, 64, 64, 66, 64, 64, 68, 68, 68, 64, 64, 64, 56, 64, 64, 60, 60, 66, 64, 62, 62, 66, 64, 64, 68, 68, 68, 68, 66, 64, 68, 68, -1]

LANDED = 3
SOURCE, BACK, TARGET, LAST = 8, 10, 11, 13


def plan_kernel(
    plan_ref, table_ref, scale_ref, bias_ref, audio_ref, text_ref,
    pair_ref, code_ref, leaf_ref, scalar_ref, own_ref, held_ref, sems,
):
    loads = [
        pltpu.make_async_copy(ref, pair_ref.at[i], sems.at[i])
        for i, ref in enumerate((audio_ref, text_ref))
    ]
    keeps = [
        pltpu.make_async_copy(pair_ref.at[i], own_ref.at[i], sems.at[2 + i]) for i in range(2)
    ]
    for copy in loads:
        copy.start()
    scalar_ref[0:1, :] = jnp.full((1, 128), scale_ref[0], jnp.float32)
    scalar_ref[1:8, :] = jnp.full((7, 128), bias_ref[0], jnp.float32)
    me = lax.axis_index("dp")
    offsets = [(plan_ref[0, r] - me) & 255 for r in range(ROUNDS)]

    def entry(distance):
        return jnp.maximum(jnp.minimum(distance, 256 - distance) - 1, 0)

    def cost(distance):
        return table_ref[entry(distance)]

    def code(transfer, source, target):
        return (
            (transfer >> 1) | (source << SOURCE) | ((transfer & 1) << BACK) | (target << TARGET)
        )

    for load, keep in zip(loads, keeps):
        load.wait()
        keep.start()
    far = jnp.int32(1 << 28)
    best = [cost(s) for s in offsets]
    parent = [jnp.int32(0)] * ROUNDS
    away = list(offsets)
    done = [jnp.int32(0)] * ROUNDS
    count = jnp.int32(0)
    for step in range(ROUNDS):
        keys = [jnp.where(done[j] == 1, far, best[j]) for j in range(ROUNDS)]
        first = (keys[0] <= keys[1]) & (keys[0] <= keys[2])
        pick = jnp.where(first, 0, jnp.where(keys[1] <= keys[2], 1, 2))

        def chosen(values):
            return jnp.where(pick == 0, values[0], jnp.where(pick == 1, values[1], values[2]))

        distance = chosen(away)
        at = chosen(offsets)
        mirrored = jnp.where(distance <= HALF, 0, 1)
        one = table_ref[HALF + entry(distance)] ^ mirrored
        two = table_ref[2 * HALF + entry(distance)]
        twice = two >= 0
        two = jnp.maximum(two, 0) ^ mirrored
        source = chosen(parent)
        if step > 0:
            source = jnp.where(source == step, LANDED, source)
        code_ref[count] = code(one, source, jnp.where(twice, 0, step + 1))
        code_ref[count + 1] = code(two, LANDED, step + 1)
        count = count + jnp.where(twice, 2, 1)
        for j in range(ROUNDS):
            done[j] = jnp.where(pick == j, 1, done[j])
            onward = (offsets[j] - at) & 255
            price = cost(onward)
            nearer = price < best[j]
            best[j] = jnp.where(nearer, price, best[j])
            parent[j] = jnp.where(nearer, step + 1, parent[j])
            away[j] = jnp.where(nearer, onward, away[j])
    code_ref[count - 1] = code_ref[count - 1] | (1 << LAST)
    leaf_ref[0] = code_ref[0] & 255
    for copy in keeps:
        copy.wait()

    @pl.when(((code_ref[0] >> BACK) & 1) == 1)
    def _():
        audio, text = pair_ref[0], pair_ref[1]
        pair_ref[0] = text
        pair_ref[1] = audio


def plan_transfers(audio, text, log_scale, bias, plan):
    return pl.pallas_call(
        plan_kernel,
        out_shape=(
            jax.ShapeDtypeStruct((2,) + audio.shape, audio.dtype),
            jax.ShapeDtypeStruct((8,), jnp.int32),
            jax.ShapeDtypeStruct((1,), jnp.int32),
            jax.ShapeDtypeStruct((8, 128), jnp.float32),
            jax.ShapeDtypeStruct((2,) + audio.shape, audio.dtype),
            jax.ShapeDtypeStruct((2 * (ROUNDS - 1),) + audio.shape, audio.dtype),
        ),
        in_specs=[SMEM, SMEM, SMEM, SMEM, ANY, ANY],
        out_specs=(VMEM, SMEM, SMEM, VMEM, ANY, ANY),
        scratch_shapes=[pltpu.SemaphoreType.DMA((4,))],
    )(plan, jnp.asarray(np.array(COST + FIRST + SECOND, np.int32)), log_scale, bias, audio, text)


def store_kernel(
    held_in, own_in, landed_ref, code_in,
    held_ref, own_ref, pair_ref, code_ref, leaf_ref, sems,
):
    codes = [code_in[i] for i in range(8)]
    back = (codes[0] >> BACK) & 1
    target = (codes[0] >> TARGET) & 3
    slot = jnp.where(target == 2, 1, 0)
    stores = [
        pltpu.make_async_copy(
            landed_ref.at[i], held_ref.at[2 * slot + (back if i == 0 else 1 - back)], sems.at[i]
        )
        for i in range(2)
    ]

    @pl.when(target > 0)
    def _():
        for copy in stores:
            copy.start()

    for i in range(7):
        code_ref[i] = codes[i + 1]
    code_ref[7] = 0
    leaf_ref[0] = (codes[1] & 255) | (((codes[1] >> LAST) & 1) << 8)
    source = (codes[1] >> SOURCE) & 3
    turn = (codes[1] >> BACK) & 1

    def load(first, second):
        loads = [
            pltpu.make_async_copy(ref, pair_ref.at[i], sems.at[2 + i])
            for i, ref in enumerate((first, second))
        ]
        for copy in loads:
            copy.start()
        for copy in loads:
            copy.wait()

    @pl.when(source == LANDED)
    def _():
        same = back == turn
        first, second = landed_ref[0], landed_ref[1]
        pair_ref[0] = jnp.where(same, first, second)
        pair_ref[1] = jnp.where(same, second, first)

    @pl.when(source == 0)
    def _():
        load(own_ref.at[turn], own_ref.at[1 - turn])

    @pl.when((source == 1) | (source == 2))
    def _():
        at = 2 * jnp.where(source == 2, 1, 0)
        load(held_ref.at[at + turn], held_ref.at[at + 1 - turn])

    @pl.when(target > 0)
    def _():
        for copy in stores:
            copy.wait()


def store_landed(held, own, landed, codes):
    return pl.pallas_call(
        store_kernel,
        out_shape=(
            jax.ShapeDtypeStruct(held.shape, held.dtype),
            jax.ShapeDtypeStruct(own.shape, own.dtype),
            jax.ShapeDtypeStruct(landed.shape, landed.dtype),
            jax.ShapeDtypeStruct((8,), jnp.int32),
            jax.ShapeDtypeStruct((1,), jnp.int32),
        ),
        in_specs=[ANY, ANY, VMEM, SMEM],
        out_specs=(ANY, ANY, VMEM, SMEM, SMEM),
        scratch_shapes=[pltpu.SemaphoreType.DMA((4,))],
        input_output_aliases={0: 0, 1: 1, 3: 3},
    )(held, own, landed, codes)


def swap_kernel(distance, pair_ref, landed_ref, send_sem, recv_sem):
    me = lax.axis_index("dp")
    partners = (lax.rem(me + distance, 256), lax.rem(me + 256 - distance, 256))
    barrier = pltpu.get_barrier_semaphore()
    for device in partners:
        pl.semaphore_signal(barrier, inc=1, device_id=(device,), device_id_type=MESH)
    pl.semaphore_wait(barrier, 2)
    copies = [
        pltpu.make_async_remote_copy(
            src_ref=pair_ref.at[i],
            dst_ref=landed_ref.at[i],
            send_sem=send_sem.at[i],
            recv_sem=recv_sem.at[i],
            device_id=(device,),
            device_id_type=MESH,
        )
        for i, device in enumerate(partners)
    ]
    for copy in copies:
        copy.start()
    for copy in copies:
        copy.wait()


def swap(leaf, pair):
    return pl.pallas_call(
        partial(swap_kernel, SHIFTS[leaf]),
        out_shape=jax.ShapeDtypeStruct(pair.shape, pair.dtype),
        in_specs=[ANY],
        out_specs=ANY,
        scratch_shapes=[pltpu.SemaphoreType.DMA((2,)), pltpu.SemaphoreType.DMA((2,))],
        compiler_params=pltpu.CompilerParams(
            collective_id=1 + leaf, has_side_effects=True, vmem_limit_bytes=MIB
        ),
    )(pair)


def unit_rows(raw):
    wide = raw.astype(jnp.float32)
    recip = lax.rsqrt(jnp.sum(wide * wide, axis=-1, keepdims=True) + EPSILON)
    wide = wide * recip
    return wide, recip, wide.astype(jnp.bfloat16)


def dot_t(a, b):
    return lax.dot_general(a, b, (((1,), (1,)), ((), ())), preferred_element_type=jnp.float32)


def project(wide, recip, grad):
    along = jnp.sum(wide * grad, axis=-1, keepdims=True)
    return recip * (grad - wide * along)


def loss_kernel(
    denominator, scalar_ref, code_ref, audio_ref, text_ref, held_in, landed_ref,
    row_ref, ga_ref, gt_ref, stats_ref, held_hbm, held_ref, sems, *scratch,
):
    me = lax.axis_index("dp")
    loads = {
        i: pltpu.make_async_copy(held_hbm.at[i], held_ref.at[i], sems.at[i]) for i in (1, 3, 0, 2)
    }
    for copy in loads.values():
        copy.start()
    count = len(STAGES)
    buffers, sends, recvs = [scratch[i * count : (i + 1) * count] for i in range(3)]
    groups = []
    for stride, peers in STAGES:
        digit = lax.rem(lax.div(me, stride), peers)
        others = []
        for k in range(1, peers):
            other = lax.rem(digit + k, peers)
            others.append((other, me + (other - digit) * stride))
        groups.append((digit, others))
    barrier = pltpu.get_barrier_semaphore()
    for _, others in groups:
        for _, device in others:
            pl.semaphore_signal(barrier, inc=1, device_id=(device,), device_id_type=MESH)

    def copies(stage):
        digit, others = groups[stage]
        return [
            pltpu.make_async_remote_copy(
                src_ref=buffers[stage].at[digit],
                dst_ref=buffers[stage].at[digit],
                send_sem=sends[stage].at[other],
                recv_sem=recvs[stage].at[digit],
                device_id=(device,),
                device_id_type=MESH,
            )
            for other, device in others
        ]

    def send(stage, value):
        buffers[stage][groups[stage][0]] = value
        for copy in copies(stage):
            copy.start()

    def receive(stage):
        digit, others = groups[stage]
        for other, device in others:
            pltpu.make_async_remote_copy(
                src_ref=buffers[stage].at[digit],
                dst_ref=buffers[stage].at[other],
                send_sem=sends[stage].at[other],
                recv_sem=recvs[stage].at[other],
                device_id=(device,),
                device_id_type=MESH,
            ).wait_recv()
        value = buffers[stage][0]
        for j in range(1, STAGES[stage][1]):
            value = value + buffers[stage][j]
        return value

    n = audio_ref.shape[0]
    scale = jnp.exp(scalar_ref[0:1, 0:1])
    bias = scalar_ref[1:2, 0:1]
    rows = lax.broadcasted_iota(jnp.int32, (n, n), 0)
    cols = lax.broadcasted_iota(jnp.int32, (n, n), 1)
    eye = (rows == cols).astype(jnp.float32)
    backwards = ((code_ref[0] >> BACK) & 1) == 1
    audio_wide, audio_recip, audio_unit = unit_rows(audio_ref[...])
    text_wide, text_recip, text_unit = unit_rows(text_ref[...])
    losses_sum = jnp.zeros((n, n), jnp.float32)
    slopes_sum = jnp.zeros((n, n), jnp.float32)
    scaled_sum = jnp.zeros((n, n), jnp.float32)
    far_texts, far_weights = [], []
    for slot in (0, 3, 1, 2):
        if slot == 0:
            far_text = text_unit
        elif slot < ROUNDS:
            loads[2 * slot - 1].wait()
            far_text = unit_rows(held_ref[2 * slot - 1])[2]
        else:
            far_text = unit_rows(jnp.where(backwards, landed_ref[0], landed_ref[1]))[2]
        scaled = scale * dot_t(audio_unit, far_text)
        logits = scaled + bias
        small = jnp.exp(-jnp.abs(logits))
        slopes = jnp.where(logits >= 0.0, 1.0, small) / (1.0 + small)
        if slot == 0:
            flipped = jnp.where(rows == cols, -logits, logits)
            slopes = slopes - eye
        else:
            flipped = logits
        losses_sum = losses_sum + (jnp.maximum(flipped, 0.0) + jnp.log1p(small))
        slopes_sum = slopes_sum + slopes
        scaled_sum = scaled_sum + slopes * scaled
        far_texts.append(far_text)
        far_weights.append((scale * slopes).astype(jnp.bfloat16))

    parts = []
    for total in (losses_sum, slopes_sum, scaled_sum):
        down = jnp.sum(total, axis=0, keepdims=True)
        parts.append(down[:, : n // 2] + down[:, n // 2 :])
    parts = jnp.concatenate(parts + [jnp.zeros((5, n // 2), jnp.float32)], axis=0)
    pl.semaphore_wait(barrier, sum(peers - 1 for _, peers in STAGES))
    send(0, parts)

    audio_grad = jnp.zeros(audio_wide.shape, jnp.float32)
    for far_text, weights in zip(far_texts, far_weights):
        audio_grad = audio_grad + jnp.dot(weights, far_text, preferred_element_type=jnp.float32)
    ga_ref[...] = project(audio_wide, audio_recip, audio_grad)
    send(1, receive(0))

    text_grad = jnp.zeros(text_wide.shape, jnp.float32)
    for slot in range(ROUNDS + 1):
        if slot == 0:
            far_audio = audio_unit
        elif slot < ROUNDS:
            loads[2 * slot - 2].wait()
            far_audio = unit_rows(held_ref[2 * slot - 2])[2]
        else:
            far_audio = unit_rows(jnp.where(backwards, landed_ref[1], landed_ref[0]))[2]
        logits = scale * dot_t(text_unit, far_audio) + bias
        small = jnp.exp(-jnp.abs(logits))
        slopes = jnp.where(logits >= 0.0, 1.0, small) / (1.0 + small)
        if slot == 0:
            slopes = slopes - eye
        weights = (scale * slopes).astype(jnp.bfloat16)
        text_grad = text_grad + jnp.dot(weights, far_audio, preferred_element_type=jnp.float32)
        if slot == 1:
            send(2, receive(1))
    gt_ref[...] = project(text_wide, text_recip, text_grad)
    folded = losses_sum[:, : n // 2] + losses_sum[:, n // 2 :]
    row_ref[...] = jnp.sum(folded.T, axis=0, keepdims=True)
    total = jnp.sum(receive(2), axis=1, keepdims=True) / denominator
    stats_ref[...] = jnp.broadcast_to(total, stats_ref.shape)
    for stage in range(len(STAGES)):
        for copy in copies(stage):
            copy.wait_send()


def loss_and_grads(denominator, scalars, codes, audio, text, held, landed):
    n, d = audio.shape
    part = (8, n // 2)
    return pl.pallas_call(
        partial(loss_kernel, denominator),
        out_shape=(
            jax.ShapeDtypeStruct((1, n), jnp.float32),
            jax.ShapeDtypeStruct((n, d), jnp.float32),
            jax.ShapeDtypeStruct((n, d), jnp.float32),
            jax.ShapeDtypeStruct(part, jnp.float32),
            jax.ShapeDtypeStruct(held.shape, held.dtype),
        ),
        in_specs=[VMEM, SMEM, VMEM, VMEM, ANY, VMEM],
        out_specs=(VMEM, VMEM, VMEM, VMEM, ANY),
        input_output_aliases={4: 4},
        scratch_shapes=[
            pltpu.VMEM(held.shape, held.dtype),
            pltpu.SemaphoreType.DMA((4,)),
        ]
        + [pltpu.VMEM((peers,) + part, jnp.float32) for _, peers in STAGES]
        + [pltpu.SemaphoreType.DMA((peers,)) for _, peers in STAGES] * 2,
        compiler_params=pltpu.CompilerParams(
            collective_id=0, has_side_effects=True, vmem_limit_bytes=40 * MIB
        ),
    )(scalars, codes, audio, text, held, landed)[:4]


def result_kernel(row_in, ga_in, gt_in, stats_in, row_ref, ga_ref, gt_ref, stats_ref, sems):
    moves = [
        pltpu.make_async_copy(src, dst, sems.at[i])
        for i, (src, dst) in enumerate(((ga_in, ga_ref), (gt_in, gt_ref)))
    ]
    for copy in moves:
        copy.start()
    row_ref[...] = row_in[...]
    for i in range(3):
        stats_ref[i] = stats_in[i, 0]
    for copy in moves:
        copy.wait()


def results(row_loss, grad_audio, grad_text, stats):
    return pl.pallas_call(
        result_kernel,
        out_shape=(
            jax.ShapeDtypeStruct(row_loss.shape, jnp.float32),
            jax.ShapeDtypeStruct(grad_audio.shape, jnp.float32),
            jax.ShapeDtypeStruct(grad_text.shape, jnp.float32),
            jax.ShapeDtypeStruct((3,), jnp.float32),
        ),
        in_specs=[VMEM] * 4,
        out_specs=(VMEM, ANY, ANY, SMEM),
        scratch_shapes=[pltpu.SemaphoreType.DMA((2,))],
        compiler_params=pltpu.CompilerParams(vmem_limit_bytes=8 * MIB),
    )(row_loss, grad_audio, grad_text, stats)


def local(audio, text, log_scale, bias, plan):
    n, d = audio.shape
    player_count = lax.axis_size("dp")
    leaves = [partial(swap, leaf) for leaf in range(len(SHIFTS))]
    pair, codes, leaf, scalars, own, held = plan_transfers(audio, text, log_scale, bias, plan)

    def transfer(state):
        held, own, pair, codes, leaf = state
        landed = lax.switch(leaf[0], leaves, pair)
        return store_landed(held, own, landed, codes)

    state = (held, own, pair, codes, leaf)
    held, _, pair, codes, leaf = lax.while_loop(lambda s: s[4][0] < 256, transfer, state)
    landed = lax.switch(leaf[0] - 256, leaves, pair)
    row_loss, grad_audio, grad_text, stats = results(
        *loss_and_grads(
            float((ROUNDS + 1) * n * n * player_count), scalars, codes, audio, text, held, landed
        )
    )
    return (row_loss.reshape(n), grad_audio, grad_text, stats)


def solution(mesh):
    return jax.shard_map(
        local,
        mesh=mesh,
        in_specs=(P("dp", None), P("dp", None), P(), P(), P("dp", None)),
        out_specs=(P("dp"), P("dp", None), P("dp", None), P()),
        check_vma=False,
    )
```

```python
from functools import partial

import jax
import jax.numpy as jnp
import numpy as np
from jax import lax
from jax.experimental import pallas as pl
from jax.experimental.pallas import tpu as pltpu
from jax.sharding import PartitionSpec as P

EPSILON = 1e-06
ROUNDS = 3
HALF = 128
STAGES = ((32, 8), (8, 4), (1, 8))
MESH = pl.DeviceIdType.MESH
MIB = 1024 * 1024
ANY = pl.BlockSpec(memory_space=pl.ANY)
VMEM = pl.BlockSpec(memory_space=pltpu.VMEM)
SMEM = pl.BlockSpec(memory_space=pltpu.SMEM)

SHIFTS = (1, 2, 5, 6, 7, 8, 9, 16, 19, 21, 23, 24, 25, 26, 28, 30, 31, 32, 33, 34, 36, 37, 41, 42, 43, 45, 46, 50, 54, 55, 57, 61, 64, 67, 128)
COST = [144, 191, 335, 382, 245, 198, 197, 194, 233, 377, 424, 396, 394, 392, 391, 307, 378, 379, 323, 397, 309, 372, 246, 181, 214, 199, 343, 284, 342, 198, 201, 155, 213, 254, 397, 302, 287, 353, 351, 349, 298, 312, 330, 474, 333, 333, 428, 363, 395, 308, 413, 399, 444, 315, 310, 336, 314, 354, 413, 396, 323, 353, 356, 267, 368, 409, 373, 457, 442, 464, 463, 461, 453, 467, 485, 507, 488, 488, 491, 506, 495, 462, 513, 513, 505, 470, 465, 448, 468, 466, 521, 525, 478, 465, 468, 421, 480, 520, 528, 568, 554, 567, 581, 549, 565, 579, 597, 630, 600, 600, 629, 623, 706, 574, 638, 633, 680, 582, 577, 562, 564, 565, 613, 686, 590, 558, 511, 367]
FIRST = [0, 2, 0, 2, 4, 6, 8, 10, 12, 0, 2, 6, 6, 6, 8, 14, 9, 7, 16, 7, 18, 3, 20, 22, 24, 26, 0, 28, 1, 30, 32, 34, 36, 38, 0, 40, 42, 6, 8, 10, 44, 46, 48, 0, 50, 52, 20, 22, 22, 54, 24, 26, 20, 56, 58, 22, 60, 26, 26, 30, 62, 30, 32, 64, 34, 34, 66, 34, 34, 6, 8, 10, 34, 34, 34, 26, 34, 34, 22, 30, 22, 34, 26, 30, 22, 34, 34, 22, 34, 26, 30, 32, 34, 30, 32, 34, 36, 38, 34, 40, 42, 27, 25, 23, 44, 46, 48, 56, 50, 52, 56, 58, 52, 54, 56, 58, 54, 56, 58, 11, 9, 7, 5, 60, 62, 3, 1, 68]
SECOND = [-1, -1, 2, 2, -1, -1, -1, -1, -1, 12, 12, 6, 8, 10, 10, -1, 22, 22, -1, 26, -1, 22, -1, -1, -1, -1, 26, -1, 30, -1, -1, -1, -1, -1, 38, -1, -1, 34, 34, 34, -1, -1, -1, 48, -1, -1, 22, 22, 24, -1, 26, 26, 30, -1, -1, 34, -1, 34, 36, 30, -1, 34, 34, -1, 36, 38, -1, 40, 42, 64, 64, 64, 44, 46, 48, 54, 50, 52, 58, 54, 60, 54, 60, 56, 62, 56, 58, 64, 60, 64, 62, 62, 62, 64, 64, 64, 64, 64, 66, 64, 64, 68, 68, 68, 64, 64, 64, 56, 64, 64, 60, 60, 66, 64, 62, 62, 66, 64, 64, 68, 68, 68, 68, 66, 64, 68, 68, -1]

LANDED = 3
SOURCE, BACK, TARGET, LAST = 8, 10, 11, 13


def plan_kernel(
    plan_ref, table_ref, scale_ref, bias_ref, audio_ref, text_ref,
    pair_ref, code_ref, leaf_ref, scalar_ref, own_ref, held_ref, sems,
):
    loads = [
        pltpu.make_async_copy(ref, pair_ref.at[i], sems.at[i])
        for i, ref in enumerate((audio_ref, text_ref))
    ]
    keeps = [
        pltpu.make_async_copy(pair_ref.at[i], own_ref.at[i], sems.at[2 + i]) for i in range(2)
    ]
    for copy in loads:
        copy.start()
    scalar_ref[0:1, :] = jnp.full((1, 128), scale_ref[0], jnp.float32)
    scalar_ref[1:8, :] = jnp.full((7, 128), bias_ref[0], jnp.float32)
    me = lax.axis_index("dp")
    offsets = [(plan_ref[0, r] - me) & 255 for r in range(ROUNDS)]

    def entry(distance):
        return jnp.maximum(jnp.minimum(distance, 256 - distance) - 1, 0)

    def cost(distance):
        return table_ref[entry(distance)]

    def code(transfer, source, target):
        return (
            (transfer >> 1) | (source << SOURCE) | ((transfer & 1) << BACK) | (target << TARGET)
        )

    for load, keep in zip(loads, keeps):
        load.wait()
        keep.start()
    far = jnp.int32(1 << 28)
    best = [cost(s) for s in offsets]
    parent = [jnp.int32(0)] * ROUNDS
    away = list(offsets)
    done = [jnp.int32(0)] * ROUNDS
    count = jnp.int32(0)
    for step in range(ROUNDS):
        keys = [jnp.where(done[j] == 1, far, best[j]) for j in range(ROUNDS)]
        first = (keys[0] <= keys[1]) & (keys[0] <= keys[2])
        pick = jnp.where(first, 0, jnp.where(keys[1] <= keys[2], 1, 2))

        def chosen(values):
            return jnp.where(pick == 0, values[0], jnp.where(pick == 1, values[1], values[2]))

        distance = chosen(away)
        at = chosen(offsets)
        mirrored = jnp.where(distance <= HALF, 0, 1)
        one = table_ref[HALF + entry(distance)] ^ mirrored
        two = table_ref[2 * HALF + entry(distance)]
        twice = two >= 0
        two = jnp.maximum(two, 0) ^ mirrored
        source = chosen(parent)
        if step > 0:
            source = jnp.where(source == step, LANDED, source)
        code_ref[count] = code(one, source, jnp.where(twice, 0, step + 1))
        code_ref[count + 1] = code(two, LANDED, step + 1)
        count = count + jnp.where(twice, 2, 1)
        for j in range(ROUNDS):
            done[j] = jnp.where(pick == j, 1, done[j])
            onward = (offsets[j] - at) & 255
            price = cost(onward)
            nearer = price < best[j]
            best[j] = jnp.where(nearer, price, best[j])
            parent[j] = jnp.where(nearer, step + 1, parent[j])
            away[j] = jnp.where(nearer, onward, away[j])
    code_ref[count - 1] = code_ref[count - 1] | (1 << LAST)
    leaf_ref[0] = code_ref[0] & 255
    for copy in keeps:
        copy.wait()

    @pl.when(((code_ref[0] >> BACK) & 1) == 1)
    def _():
        audio, text = pair_ref[0], pair_ref[1]
        pair_ref[0] = text
        pair_ref[1] = audio


def plan_transfers(audio, text, log_scale, bias, plan):
    return pl.pallas_call(
        plan_kernel,
        out_shape=(
            jax.ShapeDtypeStruct((2,) + audio.shape, audio.dtype),
            jax.ShapeDtypeStruct((8,), jnp.int32),
            jax.ShapeDtypeStruct((1,), jnp.int32),
            jax.ShapeDtypeStruct((8, 128), jnp.float32),
            jax.ShapeDtypeStruct((2,) + audio.shape, audio.dtype),
            jax.ShapeDtypeStruct((2 * (ROUNDS - 1),) + audio.shape, audio.dtype),
        ),
        in_specs=[SMEM, SMEM, SMEM, SMEM, ANY, ANY],
        out_specs=(VMEM, SMEM, SMEM, VMEM, ANY, ANY),
        scratch_shapes=[pltpu.SemaphoreType.DMA((4,))],
    )(plan, jnp.asarray(np.array(COST + FIRST + SECOND, np.int32)), log_scale, bias, audio, text)


def store_kernel(
    held_in, own_in, landed_ref, code_in,
    held_ref, own_ref, pair_ref, code_ref, leaf_ref, sems,
):
    codes = [code_in[i] for i in range(8)]
    back = (codes[0] >> BACK) & 1
    target = (codes[0] >> TARGET) & 3
    slot = jnp.where(target == 2, 1, 0)
    stores = [
        pltpu.make_async_copy(
            landed_ref.at[i], held_ref.at[2 * slot + (back if i == 0 else 1 - back)], sems.at[i]
        )
        for i in range(2)
    ]

    @pl.when(target > 0)
    def _():
        for copy in stores:
            copy.start()

    for i in range(7):
        code_ref[i] = codes[i + 1]
    code_ref[7] = 0
    leaf_ref[0] = (codes[1] & 255) | (((codes[1] >> LAST) & 1) << 8)
    source = (codes[1] >> SOURCE) & 3
    turn = (codes[1] >> BACK) & 1

    def load(first, second):
        loads = [
            pltpu.make_async_copy(ref, pair_ref.at[i], sems.at[2 + i])
            for i, ref in enumerate((first, second))
        ]
        for copy in loads:
            copy.start()
        for copy in loads:
            copy.wait()

    @pl.when(source == LANDED)
    def _():
        same = back == turn
        first, second = landed_ref[0], landed_ref[1]
        pair_ref[0] = jnp.where(same, first, second)
        pair_ref[1] = jnp.where(same, second, first)

    @pl.when(source == 0)
    def _():
        load(own_ref.at[turn], own_ref.at[1 - turn])

    @pl.when((source == 1) | (source == 2))
    def _():
        at = 2 * jnp.where(source == 2, 1, 0)
        load(held_ref.at[at + turn], held_ref.at[at + 1 - turn])

    @pl.when(target > 0)
    def _():
        for copy in stores:
            copy.wait()


def store_landed(held, own, landed, codes):
    return pl.pallas_call(
        store_kernel,
        out_shape=(
            jax.ShapeDtypeStruct(held.shape, held.dtype),
            jax.ShapeDtypeStruct(own.shape, own.dtype),
            jax.ShapeDtypeStruct(landed.shape, landed.dtype),
            jax.ShapeDtypeStruct((8,), jnp.int32),
            jax.ShapeDtypeStruct((1,), jnp.int32),
        ),
        in_specs=[ANY, ANY, VMEM, SMEM],
        out_specs=(ANY, ANY, VMEM, SMEM, SMEM),
        scratch_shapes=[pltpu.SemaphoreType.DMA((4,))],
        input_output_aliases={0: 0, 1: 1, 3: 3},
    )(held, own, landed, codes)


def swap_kernel(distance, pair_ref, landed_ref, send_sem, recv_sem):
    me = lax.axis_index("dp")
    partners = (lax.rem(me + distance, 256), lax.rem(me + 256 - distance, 256))
    barrier = pltpu.get_barrier_semaphore()
    for device in partners:
        pl.semaphore_signal(barrier, inc=1, device_id=(device,), device_id_type=MESH)
    pl.semaphore_wait(barrier, 2)
    copies = [
        pltpu.make_async_remote_copy(
            src_ref=pair_ref.at[i],
            dst_ref=landed_ref.at[i],
            send_sem=send_sem.at[i],
            recv_sem=recv_sem.at[i],
            device_id=(device,),
            device_id_type=MESH,
        )
        for i, device in enumerate(partners)
    ]
    for copy in copies:
        copy.start()
    for copy in copies:
        copy.wait()


def swap(leaf, pair):
    return pl.pallas_call(
        partial(swap_kernel, SHIFTS[leaf]),
        out_shape=jax.ShapeDtypeStruct(pair.shape, pair.dtype),
        in_specs=[ANY],
        out_specs=ANY,
        scratch_shapes=[pltpu.SemaphoreType.DMA((2,)), pltpu.SemaphoreType.DMA((2,))],
        compiler_params=pltpu.CompilerParams(
            collective_id=1 + leaf, has_side_effects=True, vmem_limit_bytes=MIB
        ),
    )(pair)


def unit_rows(raw):
    wide = raw.astype(jnp.float32)
    recip = lax.rsqrt(jnp.sum(wide * wide, axis=-1, keepdims=True) + EPSILON)
    wide = wide * recip
    return wide, recip, wide.astype(jnp.bfloat16)


def dot_t(a, b):
    return lax.dot_general(a, b, (((1,), (1,)), ((), ())), preferred_element_type=jnp.float32)


def project(wide, recip, grad):
    along = jnp.sum(wide * grad, axis=-1, keepdims=True)
    return recip * (grad - wide * along)


def loss_kernel(
    denominator, scalar_ref, code_ref, audio_ref, text_ref, held_in, landed_ref,
    row_ref, ga_ref, gt_ref, stats_ref, held_hbm, held_ref, sems, *scratch,
):
    me = lax.axis_index("dp")
    loads = {
        i: pltpu.make_async_copy(held_hbm.at[i], held_ref.at[i], sems.at[i]) for i in (1, 3, 0, 2)
    }
    for copy in loads.values():
        copy.start()
    count = len(STAGES)
    buffers, sends, recvs = [scratch[i * count : (i + 1) * count] for i in range(3)]
    groups = []
    for stride, peers in STAGES:
        digit = lax.rem(lax.div(me, stride), peers)
        others = []
        for k in range(1, peers):
            other = lax.rem(digit + k, peers)
            others.append((other, me + (other - digit) * stride))
        groups.append((digit, others))
    barrier = pltpu.get_barrier_semaphore()
    for _, others in groups:
        for _, device in others:
            pl.semaphore_signal(barrier, inc=1, device_id=(device,), device_id_type=MESH)

    def copies(stage):
        digit, others = groups[stage]
        return [
            pltpu.make_async_remote_copy(
                src_ref=buffers[stage].at[digit],
                dst_ref=buffers[stage].at[digit],
                send_sem=sends[stage].at[other],
                recv_sem=recvs[stage].at[digit],
                device_id=(device,),
                device_id_type=MESH,
            )
            for other, device in others
        ]

    def send(stage, value):
        buffers[stage][groups[stage][0]] = value
        for copy in copies(stage):
            copy.start()

    def receive(stage):
        digit, others = groups[stage]
        for other, device in others:
            pltpu.make_async_remote_copy(
                src_ref=buffers[stage].at[digit],
                dst_ref=buffers[stage].at[other],
                send_sem=sends[stage].at[other],
                recv_sem=recvs[stage].at[other],
                device_id=(device,),
                device_id_type=MESH,
            ).wait_recv()
        value = buffers[stage][0]
        for j in range(1, STAGES[stage][1]):
            value = value + buffers[stage][j]
        return value

    n = audio_ref.shape[0]
    scale = jnp.exp(scalar_ref[0:1, 0:1])
    bias = scalar_ref[1:2, 0:1]
    rows = lax.broadcasted_iota(jnp.int32, (n, n), 0)
    cols = lax.broadcasted_iota(jnp.int32, (n, n), 1)
    eye = (rows == cols).astype(jnp.float32)
    backwards = ((code_ref[0] >> BACK) & 1) == 1
    audio_wide, audio_recip, audio_unit = unit_rows(audio_ref[...])
    text_wide, text_recip, text_unit = unit_rows(text_ref[...])
    losses_sum = jnp.zeros((n, n), jnp.float32)
    slopes_sum = jnp.zeros((n, n), jnp.float32)
    scaled_sum = jnp.zeros((n, n), jnp.float32)
    far_texts, far_weights = [], []
    for slot in (0, 3, 1, 2):
        if slot == 0:
            far_text = text_unit
        elif slot < ROUNDS:
            loads[2 * slot - 1].wait()
            far_text = unit_rows(held_ref[2 * slot - 1])[2]
        else:
            far_text = unit_rows(jnp.where(backwards, landed_ref[0], landed_ref[1]))[2]
        scaled = scale * dot_t(audio_unit, far_text)
        logits = scaled + bias
        small = jnp.exp(-jnp.abs(logits))
        slopes = jnp.where(logits >= 0.0, 1.0, small) / (1.0 + small)
        if slot == 0:
            flipped = jnp.where(rows == cols, -logits, logits)
            slopes = slopes - eye
        else:
            flipped = logits
        losses_sum = losses_sum + (jnp.maximum(flipped, 0.0) + jnp.log1p(small))
        slopes_sum = slopes_sum + slopes
        scaled_sum = scaled_sum + slopes * scaled
        far_texts.append(far_text)
        far_weights.append((scale * slopes).astype(jnp.bfloat16))

    parts = []
    for total in (losses_sum, slopes_sum, scaled_sum):
        down = jnp.sum(total, axis=0, keepdims=True)
        parts.append(down[:, : n // 2] + down[:, n // 2 :])
    parts = jnp.concatenate(parts + [jnp.zeros((5, n // 2), jnp.float32)], axis=0)
    pl.semaphore_wait(barrier, sum(peers - 1 for _, peers in STAGES))
    send(0, parts)

    audio_grad = jnp.zeros(audio_wide.shape, jnp.float32)
    for far_text, weights in zip(far_texts, far_weights):
        audio_grad = audio_grad + jnp.dot(weights, far_text, preferred_element_type=jnp.float32)
    ga_ref[...] = project(audio_wide, audio_recip, audio_grad)
    send(1, receive(0))

    text_grad = jnp.zeros(text_wide.shape, jnp.float32)
    for slot in range(ROUNDS + 1):
        if slot == 0:
            far_audio = audio_unit
        elif slot < ROUNDS:
            loads[2 * slot - 2].wait()
            far_audio = unit_rows(held_ref[2 * slot - 2])[2]
        else:
            far_audio = unit_rows(jnp.where(backwards, landed_ref[1], landed_ref[0]))[2]
        logits = scale * dot_t(text_unit, far_audio) + bias
        small = jnp.exp(-jnp.abs(logits))
        slopes = jnp.where(logits >= 0.0, 1.0, small) / (1.0 + small)
        if slot == 0:
            slopes = slopes - eye
        weights = (scale * slopes).astype(jnp.bfloat16)
        text_grad = text_grad + jnp.dot(weights, far_audio, preferred_element_type=jnp.float32)
        if slot == 1:
            send(2, receive(1))
    gt_ref[...] = project(text_wide, text_recip, text_grad)
    folded = losses_sum[:, : n // 2] + losses_sum[:, n // 2 :]
    row_ref[...] = jnp.sum(folded.T, axis=0, keepdims=True)
    total = jnp.sum(receive(2), axis=1, keepdims=True) / denominator
    stats_ref[...] = jnp.broadcast_to(total, stats_ref.shape)
    for stage in range(len(STAGES)):
        for copy in copies(stage):
            copy.wait_send()


def loss_and_grads(denominator, scalars, codes, audio, text, held, landed):
    n, d = audio.shape
    part = (8, n // 2)
    return pl.pallas_call(
        partial(loss_kernel, denominator),
        out_shape=(
            jax.ShapeDtypeStruct((1, n), jnp.float32),
            jax.ShapeDtypeStruct((n, d), jnp.float32),
            jax.ShapeDtypeStruct((n, d), jnp.float32),
            jax.ShapeDtypeStruct(part, jnp.float32),
            jax.ShapeDtypeStruct(held.shape, held.dtype),
        ),
        in_specs=[VMEM, SMEM, VMEM, VMEM, ANY, VMEM],
        out_specs=(VMEM, VMEM, VMEM, VMEM, ANY),
        input_output_aliases={4: 4},
        scratch_shapes=[
            pltpu.VMEM(held.shape, held.dtype),
            pltpu.SemaphoreType.DMA((4,)),
        ]
        + [pltpu.VMEM((peers,) + part, jnp.float32) for _, peers in STAGES]
        + [pltpu.SemaphoreType.DMA((peers,)) for _, peers in STAGES] * 2,
        compiler_params=pltpu.CompilerParams(
            collective_id=0, has_side_effects=True, vmem_limit_bytes=40 * MIB
        ),
    )(scalars, codes, audio, text, held, landed)[:4]


def result_kernel(row_in, ga_in, gt_in, stats_in, row_ref, ga_ref, gt_ref, stats_ref, sems):
    moves = [
        pltpu.make_async_copy(src, dst, sems.at[i])
        for i, (src, dst) in enumerate(((ga_in, ga_ref), (gt_in, gt_ref)))
    ]
    for copy in moves:
        copy.start()
    row_ref[...] = row_in[...]
    for i in range(3):
        stats_ref[i] = stats_in[i, 0]
    for copy in moves:
        copy.wait()


def results(row_loss, grad_audio, grad_text, stats):
    return pl.pallas_call(
        result_kernel,
        out_shape=(
            jax.ShapeDtypeStruct(row_loss.shape, jnp.float32),
            jax.ShapeDtypeStruct(grad_audio.shape, jnp.float32),
            jax.ShapeDtypeStruct(grad_text.shape, jnp.float32),
            jax.ShapeDtypeStruct((3,), jnp.float32),
        ),
        in_specs=[VMEM] * 4,
        out_specs=(VMEM, ANY, ANY, SMEM),
        scratch_shapes=[pltpu.SemaphoreType.DMA((2,))],
        compiler_params=pltpu.CompilerParams(vmem_limit_bytes=8 * MIB),
    )(row_loss, grad_audio, grad_text, stats)


def local(audio, text, log_scale, bias, plan):
    n, d = audio.shape
    player_count = lax.axis_size("dp")
    leaves = [partial(swap, leaf) for leaf in range(len(SHIFTS))]
    pair, codes, leaf, scalars, own, held = plan_transfers(audio, text, log_scale, bias, plan)

    def transfer(state):
        held, own, pair, codes, leaf = state
        landed = lax.switch(leaf[0], leaves, pair)
        return store_landed(held, own, landed, codes)

    state = (held, own, pair, codes, leaf)
    held, _, pair, codes, leaf = lax.while_loop(lambda s: s[4][0] < 256, transfer, state)
    landed = lax.switch(leaf[0] - 256, leaves, pair)
    row_loss, grad_audio, grad_text, stats = results(
        *loss_and_grads(
            float((ROUNDS + 1) * n * n * player_count), scalars, codes, audio, text, held, landed
        )
    )
    return (row_loss.reshape(n), grad_audio, grad_text, stats)


def solution(mesh):
    return jax.shard_map(
        local,
        mesh=mesh,
        in_specs=(P("dp", None), P("dp", None), P(), P(), P("dp", None)),
        out_specs=(P("dp"), P("dp", None), P("dp", None), P()),
        check_vma=False,
    )
```
